256 devices in a mesh: lat: 16 (over z_hi, y), lon: 2 (over z_lo), dp: 8 (over x, core).
Axes of the slice: x: 4, y: 4, z: 8 (z_hi: 4, z_lo: 2; z = z_hi * 2 + z_lo), core: 2. Of those that a mesh axis runs over, the one named last changes fastest.
Arguments:
- inputs: bfloat16 [8, 384, 128, 768], P('dp', 'lat', 'lon'), may hold values from -6 to 6
- cotangent: bfloat16 [8, 384, 128, 768], P('dp', 'lat', 'lon'), may hold values from -6 to 6
- weight: bfloat16 [384, 2, 128, 128], P(('lat', 'dp'), None, 'lon'), may hold values from -0.375 to 0.375
Outputs:
- input_grad: bfloat16 [8, 384, 128, 768], P('dp', 'lat', 'lon')
- weight_grad: float32 [384, 2, 128, 128], P(('lat', 'dp'), None, 'lon')
The draws below stay inside these ranges and needn't reach their ends.
All inputs are finite; a program needn't handle non-finite values.
Results may differ from the reference program's by a relative error of at most 0.013.
Values may be sent and summed in bfloat16 or wider, within the bound.
A program may use at most 128 MiB of HBM per device.

```python
import math
import jax
import jax.numpy as jnp
from jax import lax

L = 384
NLON = 768
NLAT = 384
C = 128
B = 8


def shard_levels(own_key, extent, cuts, low, high):
    factor_of, own = 1.0, jax.random.fold_in(own_key, 6)
    for dim, parts in cuts:
        draws = jnp.exp(jax.random.uniform(jax.random.fold_in(own, dim), (parts,), jnp.float32, low / len(cuts), high / len(cuts)))
        factor_of = factor_of * jnp.repeat(draws, extent[dim] // parts).reshape([-1 if axis == dim else 1 for axis in range(len(extent))])
    return factor_of


def centred(own_key, extent, scale, limit, shards=(), kind=jnp.bfloat16):
    values = jax.random.normal(own_key, extent, jnp.float32) * scale
    if len(shards) > 0:
        values = shard_levels(own_key, extent, shards, -0.22, 0.18) * values
    return jnp.clip(values, min=-limit, max=limit).astype(kind)


def setup_inputs(seed: int = 0) -> dict:
    arg_keys = jax.random.split(jax.random.key(seed), 4)
    return {
        "inputs": centred(arg_keys[0], (B, NLAT, C, NLON), 1.0, 6.0, ((0, 8), (1, 16), (2, 2))),
        "cotangent": centred(arg_keys[1], (B, NLAT, C, NLON), 1.0, 6.0, ((0, 8), (1, 16), (2, 2))),
        "weight": centred(arg_keys[2], (L, 2, C, C), (2 * C) ** -0.5, 0.375, ((0, 128), (2, 2))),
    }


def legendre_table(orders, lat_count, degrees):
    lat_index = jnp.arange(lat_count, dtype=jnp.float32)
    colatitude = math.pi * (lat_index + 0.5) / lat_count
    cosine = jnp.cos(colatitude)[None, :]
    sine_v = jnp.sin(colatitude)[None, :]
    step_nums = jnp.arange(1, degrees, dtype=jnp.float32)
    cumlog = jnp.concatenate([jnp.zeros((1,), jnp.float32), jnp.cumsum(jnp.log1p(-0.5 / step_nums))])
    selector = (orders[:, None] == jnp.arange(degrees, dtype=jnp.int32)[None, :]).astype(jnp.float32)
    order_log = lax.optimization_barrier(jnp.sum(selector * cumlog[None, :], axis=1))
    order_f = orders.astype(jnp.float32)[:, None]
    log_start = 0.5 * (jnp.log(2.0 * order_f + 1.0) - math.log(4.0 * math.pi) + order_log[:, None]) + order_f * jnp.log(sine_v)
    shift_up = jnp.clip(-log_start - 60.0, 0.0, 80.0)
    seed_row = jnp.exp(log_start + shift_up)
    unscale = jnp.exp(-shift_up)

    def advance(state_pair, degree):
        previous, before_prev = state_pair
        degree_f = degree.astype(jnp.float32)
        upward = jnp.sqrt(jnp.maximum(4.0 * degree_f * degree_f - 1.0, 1.0) / jnp.maximum(degree_f * degree_f - order_f * order_f, 1.0))
        lower_deg = degree_f - 1.0
        backward = jnp.sqrt(jnp.maximum(lower_deg * lower_deg - order_f * order_f, 0.0) / jnp.maximum(4.0 * lower_deg * lower_deg - 1.0, 1.0))
        recurred = upward * (cosine * previous - backward * before_prev)
        fresh_row = jnp.where(degree < orders[:, None], 0.0, jnp.where(degree == orders[:, None], seed_row, recurred))
        return ((fresh_row, previous), fresh_row * unscale)
    zero_rows = jnp.zeros(seed_row.shape, jnp.float32)
    _, table_rows = lax.scan(advance, (zero_rows, zero_rows), jnp.arange(degrees, dtype=jnp.int32), unroll=16)
    return jnp.transpose(table_rows, (1, 0, 2)).astype(jnp.bfloat16)

def fourier_table(lon_count, orders_count):
    longitude = jnp.arange(lon_count, dtype=jnp.int32)
    orders = jnp.arange(orders_count, dtype=jnp.int32)
    phase = (longitude[:, None] * orders[None, :] % lon_count).astype(jnp.float32) * (2.0 * math.pi / lon_count)
    return (jnp.stack([jnp.cos(phase), -jnp.sin(phase)], axis=1) / math.sqrt(lon_count)).astype(jnp.bfloat16)

def quad_weights(lat_count):
    lat_index = jnp.arange(lat_count, dtype=jnp.float32)
    colatitude = math.pi * (lat_index + 0.5) / lat_count
    return 2.0 * math.pi * jnp.sin(colatitude) / math.sqrt(lat_count)

def reference(inputs, cotangent, weight):
    highest_precision = lax.Precision.HIGHEST
    fourier = fourier_table(NLON, L).astype(jnp.float32)
    quad_w = quad_weights(NLAT)
    real_weight = weight[:, 0].astype(jnp.float32)
    imaginary_weight = weight[:, 1].astype(jnp.float32)
    block_len = 32

    def one_sample(grad_sum, sample_pair):
        field_in, field_out = sample_pair
        spec_in = jnp.einsum('jck,krm->mjrc', field_in.astype(jnp.float32), fourier, precision=highest_precision)
        weighted = (spec_in * quad_w[None, :, None, None]).astype(jnp.bfloat16)
        spec_out = jnp.einsum('jck,krm->mjrc', field_out.astype(jnp.float32), fourier, precision=highest_precision).astype(jnp.bfloat16)

        def one_block(block_sum, block_no):
            orders = (block_no * block_len + jnp.arange(block_len, dtype=jnp.int32)).astype(jnp.int32)
            legendre = legendre_table(orders, NLAT, L).astype(jnp.float32)
            start_row = (block_no * block_len).astype(jnp.int32)
            in_block = lax.dynamic_slice_in_dim(weighted, start_row, block_len, 0).astype(jnp.float32)
            out_block = lax.dynamic_slice_in_dim(spec_out, start_row, block_len, 0).astype(jnp.float32)
            coeffs = jnp.einsum('mlj,mjrc->mlrc', legendre, in_block, precision=highest_precision).astype(jnp.bfloat16).astype(jnp.float32)
            factor = jnp.where(orders == 0, 1.0, 2.0) / math.sqrt(NLAT)
            grad_spec = (jnp.einsum('mlj,mjrc->mlrc', legendre, out_block, precision=highest_precision) * factor[:, None, None, None]).astype(jnp.bfloat16).astype(jnp.float32)
            rotated = jnp.stack([grad_spec[:, :, 1], -grad_spec[:, :, 0]], axis=2)
            block_grad = jnp.stack([jnp.einsum('mlrc,mlro->lco', coeffs, grad_spec, precision=highest_precision), jnp.einsum('mlrc,mlro->lco', coeffs, rotated, precision=highest_precision)], axis=1)
            real_gradient = grad_spec[:, :, 0]
            imaginary_gradient = grad_spec[:, :, 1]
            mixed_real_part = jnp.einsum('uyp,yqp->uyq', real_gradient, real_weight, precision=highest_precision) + jnp.einsum('uyp,yqp->uyq', imaginary_gradient, imaginary_weight, precision=highest_precision)
            mixed_imaginary_part = jnp.einsum('uyp,yqp->uyq', imaginary_gradient, real_weight, precision=highest_precision) - jnp.einsum('uyp,yqp->uyq', real_gradient, imaginary_weight, precision=highest_precision)
            mixed_spec = jnp.stack([mixed_real_part, mixed_imaginary_part], axis=2).astype(jnp.bfloat16).astype(jnp.float32)
            grid_spec = (jnp.einsum('mlj,mlrc->mjrc', legendre, mixed_spec, precision=highest_precision) * quad_w[None, :, None, None]).astype(jnp.bfloat16)
            return (block_sum + block_grad, grid_spec)
        grad_sum, grid_blocks = lax.scan(one_block, grad_sum, jnp.arange(L // block_len, dtype=jnp.int32))
        grid_all = grid_blocks.reshape(L, NLAT, 2, C).astype(jnp.float32)
        grad_field = jnp.einsum('mjrc,krm->jck', grid_all, fourier, precision=highest_precision).astype(jnp.bfloat16)
        return (grad_sum, grad_field)
    grad_total, input_grad = lax.scan(one_sample, jnp.zeros((L, 2, C, C), jnp.float32), (inputs, cotangent))
    return (input_grad, grad_total / B)
```

```python
import math

import jax
import jax.numpy as jnp
import numpy as np
from jax import lax
from jax.experimental import pallas as pl
from jax.experimental.pallas import tpu as pltpu
from jax.sharding import Mesh
from jax.sharding import PartitionSpec as P

L = 384
NLON = 768
NLAT = 384
C = 128
OWNERS = 32
SLOTS = 12
JD = 24
PAIR_ROWS = 96
MIB = 1024 * 1024
F32 = jnp.float32
BF16 = jnp.bfloat16
ORDER_AXES = ("zh", "y", "lon")
DEGREE_AXES = ("y", "dp")


def order_of(owner, slot):
    half = slot // 2
    return 64 * half + owner if slot % 2 == 0 else 64 * half + 63 - owner


def pair_index():
    table, count = {}, 0
    for slot in range(SLOTS):
        for group in range(slot // 3, 4):
            for i in range(3):
                table[slot, group, i] = count
                count += 1
    return table


PAIRS = pair_index()


def fourier_rows():
    orders = np.array([order_of(o, k) for o in range(OWNERS) for k in range(SLOTS)], np.int64)
    phase = (orders[:, None] * np.arange(NLON)[None, :] % NLON) * (2.0 * math.pi / NLON)
    rows = np.concatenate([np.cos(phase), -np.sin(phase)], axis=0) / math.sqrt(NLON)
    return rows.astype(np.float32).astype(jnp.bfloat16)


def params(limit):
    return pltpu.CompilerParams(vmem_limit_bytes=limit * MIB)


def vmem_spec():
    return pl.BlockSpec(memory_space=pltpu.VMEM)


def low_half(shape):
    return lax.broadcasted_iota(jnp.int32, shape, len(shape) - 1) < 64


def dft_kernel(x_ref, table_ref, scale_ref, out_ref, held):
    step = pl.program_id(0)
    x = x_ref[...].reshape(128, NLON)
    spec = lax.dot_general(
        table_ref[...], x, (((1,), (1,)), ((), ())), preferred_element_type=F32
    )
    real, imag = spec[:L], spec[L:]
    low = low_half((L, 128))
    even = jnp.where(low, real, pltpu.roll(imag, 64, 1))
    odd = jnp.where(low, pltpu.roll(real, 64, 1), imag)
    scale = scale_ref[...]
    held[pl.ds(2 * step, L, stride=JD), :] = even * scale[0]
    held[pl.ds(2 * step + 1, L, stride=JD), :] = odd * scale[1]

    @pl.when(step == JD // 2 - 1)
    def _():
        def body(o, _):
            start = pl.multiple_of(o * 288, 288)
            out_ref[o] = held[pl.ds(start, 288), :].astype(BF16)
            return 0

        lax.fori_loop(0, OWNERS, body, 0)


def dft(x, table, scale):
    return pl.pallas_call(
        dft_kernel,
        grid=(JD // 2,),
        in_specs=[
            pl.BlockSpec((2, 64, NLON), lambda s: (s, 0, 0)),
            pl.BlockSpec((2 * L, NLON), lambda s: (0, 0)),
            pl.BlockSpec((2, 1, 128), lambda s: (s, 0, 0)),
        ],
        out_specs=pl.BlockSpec((OWNERS, 288, 128), lambda s: (0, 0, 0)),
        out_shape=jax.ShapeDtypeStruct((OWNERS, 288, 128), BF16),
        scratch_shapes=[pltpu.VMEM((L * JD, 128), F32)],
        compiler_params=params(40),
        cost_estimate=pl.CostEstimate(
            flops=2 * 1536 * 768 * 768, bytes_accessed=6_000_000, transcendentals=0
        ),
        name="dft",
    )(x, table, scale)


def legendre_kernel(order_ref, seed_ref, unscale_ref, cos_ref, up_ref, down_ref, out_ref, held):
    order = order_ref[...]
    cosine = cos_ref[...]

    def advance(degree, row, previous, before):
        up = up_ref[degree]
        down = down_ref[degree]
        fresh = []
        for c in range(3):
            lanes = slice(128 * c, 128 * c + 128)
            value = up * (cosine[:, lanes] * previous[c] - down * before[c])
            value = jnp.where(order == degree, seed_ref[:, lanes], value)
            value = jnp.where(order > degree, 0.0, value)
            held[c, pl.ds(row, 16, stride=L), :] = value * unscale_ref[:, lanes]
            fresh.append(value)
        return fresh, previous

    def body(step, carry):
        previous, before = list(carry[:3]), list(carry[3:])
        group = step // 32
        d = step - 32 * group
        for i in range(3):
            previous, before = advance(3 * step + i, 96 * group + 32 * i + d, previous, before)
        return tuple(previous) + tuple(before)

    zero = jnp.zeros((16, 128), F32)
    lax.fori_loop(0, L // 3, body, (zero,) * 6)

    def convert(k, _):
        start = pl.multiple_of(k * L, L)
        for c in range(3):
            out_ref[pl.ds(start, L), 128 * c : 128 * c + 128] = held[
                c, pl.ds(start, L), :
            ].astype(BF16)
        return 0

    lax.fori_loop(0, SLOTS, convert, 0)


def legendre(owner):
    lat_index = jnp.arange(NLAT, dtype=F32)
    colatitude = math.pi * (lat_index + 0.5) / NLAT
    cosine = jnp.cos(colatitude)[None, :]
    sine_v = jnp.sin(colatitude)[None, :]
    slots = jnp.arange(16, dtype=jnp.int32)
    orders = jnp.where(slots % 2 == 0, 64 * (slots // 2) + owner, 64 * (slots // 2) + 63 - owner)
    orders = jnp.minimum(orders, L - 1)
    step_nums = np.arange(1, L, dtype=np.float64)
    cumlog = np.concatenate([np.zeros(1), np.cumsum(np.log1p(-0.5 / step_nums))]).astype(np.float32)
    selector = (orders[:, None] == jnp.arange(L, dtype=jnp.int32)[None, :]).astype(F32)
    order_log = jnp.sum(selector * cumlog[None, :], axis=1)
    order_f = orders.astype(F32)[:, None]
    log_start = 0.5 * (
        jnp.log(2.0 * order_f + 1.0) - math.log(4.0 * math.pi) + order_log[:, None]
    ) + order_f * jnp.log(sine_v)
    shift_up = jnp.clip(-log_start - 60.0, 0.0, 80.0)
    seed_row = jnp.exp(log_start + shift_up)
    unscale = jnp.exp(-shift_up)
    degree_f = jnp.arange(L, dtype=F32)[:, None]
    order_g = orders.astype(F32)[None, :]
    upward = jnp.sqrt(
        jnp.maximum(4.0 * degree_f * degree_f - 1.0, 1.0)
        / jnp.maximum(degree_f * degree_f - order_g * order_g, 1.0)
    )
    lower = degree_f - 1.0
    backward = jnp.sqrt(
        jnp.maximum(lower * lower - order_g * order_g, 0.0)
        / jnp.maximum(4.0 * lower * lower - 1.0, 1.0)
    )
    wide = (L, 16, 128)
    return pl.pallas_call(
        legendre_kernel,
        in_specs=[vmem_spec()] * 6,
        out_specs=vmem_spec(),
        out_shape=jax.ShapeDtypeStruct((SLOTS * L, NLAT), BF16),
        scratch_shapes=[pltpu.VMEM((3, 16 * L, 128), F32)],
        compiler_params=params(48),
        cost_estimate=pl.CostEstimate(
            flops=10 * 16 * 384 * 384, bytes_accessed=10_000_000, transcendentals=0
        ),
        name="legendre",
    )(
        jnp.broadcast_to(orders[:, None], (16, 128)),
        seed_row,
        unscale,
        jnp.broadcast_to(cosine, (16, NLAT)),
        jnp.broadcast_to(upward[:, :, None], wide),
        jnp.broadcast_to(backward[:, :, None], wide),
    )


def widen(src_ref, held, rows):
    def body(o, _):
        start = pl.multiple_of(o * rows, rows)
        held[pl.ds(start, rows), :] = src_ref[o].astype(F32)
        return 0

    lax.fori_loop(0, OWNERS, body, 0)


def narrow(held, out_ref, rows):
    def body(o, _):
        start = pl.multiple_of(o * rows, rows)
        out_ref[o] = held[pl.ds(start, rows), :].astype(BF16)
        return 0

    lax.fori_loop(0, OWNERS, body, 0)


def analyse_kernel(spec_ref, table_ref, factor_ref, out_ref, field, packed):
    widen(spec_ref, field, 288)
    packed[...] = jnp.zeros_like(packed)
    for k in range(SLOTS):
        first = k // 3
        columns = []
        for lon in range(2):
            pieces = [
                field[(2 * s + lon) * 288 + k * JD : (2 * s + lon) * 288 + k * JD + JD, :]
                for s in range(16)
            ]
            columns.append(jnp.concatenate(pieces, axis=0).astype(BF16))
        data = jnp.concatenate(columns, axis=1)
        rows = table_ref[k * L + 96 * first : (k + 1) * L, :]
        result = jnp.dot(rows, data, preferred_element_type=F32) * factor_ref[k : k + 1, :]
        for group in range(first, 4):
            for i in range(3):
                at = ((group - first) * 3 + i) * 32
                for lon in range(2):
                    row = lon * PAIR_ROWS + PAIRS[k, group, i]
                    packed[pl.ds(row, 32, stride=192), :] = result[
                        at : at + 32, 128 * lon : 128 * lon + 128
                    ]
    narrow(packed, out_ref, 192)


def analyse(spec, table, factor, name):
    return pl.pallas_call(
        analyse_kernel,
        in_specs=[vmem_spec()] * 3,
        out_specs=vmem_spec(),
        out_shape=jax.ShapeDtypeStruct((OWNERS, 192, 128), BF16),
        scratch_shapes=[pltpu.VMEM((OWNERS * 288, 128), F32), pltpu.VMEM((OWNERS * 192, 128), F32)],
        compiler_params=params(48),
        cost_estimate=pl.CostEstimate(
            flops=2 * 12 * 384 * 384 * 256, bytes_accessed=8_000_000, transcendentals=0
        ),
        name=name,
    )(spec, table, factor)


def degree_rows(held, group, i):
    parts = []
    for lon in range(2):
        pieces = [
            held[pl.ds(lon * PAIR_ROWS + PAIRS[k, group, i], 32, stride=192), :]
            for k in range(3 * group + 3)
        ]
        parts.append(jnp.concatenate(pieces, axis=0).astype(BF16))
    return jnp.concatenate(parts, axis=1)


def mix_kernel(grad_ref, weight_ref, out_ref, held, packed):
    widen(grad_ref, held, 192)
    packed[...] = jnp.zeros_like(packed)
    for group in range(4):
        for i in range(3):
            rows = degree_rows(held, group, i)
            mixed = lax.dot_general(
                rows,
                weight_ref[group * 3 + i],
                (((1,), (1,)), ((), ())),
                preferred_element_type=F32,
            )
            for k in range(3 * group + 3):
                for lon in range(2):
                    row = lon * PAIR_ROWS + PAIRS[k, group, i]
                    packed[pl.ds(row, 32, stride=192), :] = mixed[
                        32 * k : 32 * k + 32, 128 * lon : 128 * lon + 128
                    ]
    narrow(packed, out_ref, 192)


def mix(grads, weights):
    return pl.pallas_call(
        mix_kernel,
        in_specs=[vmem_spec()] * 2,
        out_specs=vmem_spec(),
        out_shape=jax.ShapeDtypeStruct((OWNERS, 192, 128), BF16),
        scratch_shapes=[pltpu.VMEM((OWNERS * 192, 128), F32)] * 2,
        compiler_params=params(40),
        cost_estimate=pl.CostEstimate(
            flops=2 * 2880 * 256 * 256, bytes_accessed=5_000_000, transcendentals=0
        ),
        name="mix",
    )(grads, weights)


def weight_grad_kernel(coeff_ref, grad_ref, out_ref, held_c, held_g):
    widen(coeff_ref, held_c, 192)
    widen(grad_ref, held_g, 192)
    low = low_half((64, 128))
    for group in range(4):
        for i in range(3):
            coeffs = degree_rows(held_c, group, i)
            grads = degree_rows(held_g, group, i)
            product = lax.dot_general(
                coeffs, grads, (((0,), (0,)), ((), ())), preferred_element_type=F32
            ) * 0.125
            for lon in range(2):
                turned = []
                for half in range(2):
                    lanes = slice(128 * half, 128 * half + 128)
                    with_real = product[128 * lon : 128 * lon + 64, lanes]
                    with_imag = pltpu.roll(product[128 * lon + 64 : 128 * lon + 128, lanes], 64, 1)
                    turned.append(jnp.where(low, with_real + with_imag, with_real - with_imag))
                first, second = turned
                out_ref[2 * group + lon, 128 * i : 128 * i + 64, :] = jnp.where(
                    low, first, pltpu.roll(second, 64, 1)
                )
                out_ref[2 * group + lon, 128 * i + 64 : 128 * i + 128, :] = jnp.where(
                    low, pltpu.roll(first, 64, 1), second
                )


def weight_grads(coeffs, grads):
    return pl.pallas_call(
        weight_grad_kernel,
        in_specs=[vmem_spec()] * 2,
        out_specs=vmem_spec(),
        out_shape=jax.ShapeDtypeStruct((8, 384, 128), F32),
        scratch_shapes=[pltpu.VMEM((OWNERS * 192, 128), F32)] * 2,
        compiler_params=params(40),
        cost_estimate=pl.CostEstimate(
            flops=2 * 2880 * 256 * 256, bytes_accessed=5_000_000, transcendentals=0
        ),
        name="weight_grads",
    )(coeffs, grads)


def synthesise_kernel(mixed_ref, table_ref, quad_ref, out_ref, held, grid):
    widen(mixed_ref, held, 192)
    for k in range(SLOTS):
        first = k // 3
        parts = []
        for lon in range(2):
            pieces = [
                held[pl.ds(lon * PAIR_ROWS + PAIRS[k, group, i], 32, stride=192), :]
                for group in range(first, 4)
                for i in range(3)
            ]
            parts.append(jnp.concatenate(pieces, axis=0).astype(BF16))
        data = jnp.concatenate(parts, axis=1)
        rows = table_ref[k * L + 96 * first : (k + 1) * L, :]
        result = lax.dot_general(
            rows, data, (((0,), (0,)), ((), ())), preferred_element_type=F32
        )
        for lon in range(2):
            scaled = result[:, 128 * lon : 128 * lon + 128] * quad_ref[...]
            for s in range(16):
                at = (2 * s + lon) * 288 + k * JD
                grid[at : at + JD, :] = scaled[s * JD : s * JD + JD]
    narrow(grid, out_ref, 288)


def synthesise(mixed, table, quad):
    return pl.pallas_call(
        synthesise_kernel,
        in_specs=[vmem_spec()] * 3,
        out_specs=vmem_spec(),
        out_shape=jax.ShapeDtypeStruct((OWNERS, 288, 128), BF16),
        scratch_shapes=[pltpu.VMEM((OWNERS * 192, 128), F32), pltpu.VMEM((OWNERS * 288, 128), F32)],
        compiler_params=params(48),
        cost_estimate=pl.CostEstimate(
            flops=2 * 12 * 384 * 384 * 256, bytes_accessed=8_000_000, transcendentals=0
        ),
        name="synthesise",
    )(mixed, table, quad)


def inverse_kernel(spec_ref, table_ref, out_ref, held, turned):
    step = pl.program_id(0)

    @pl.when(step == 0)
    def _():
        widen(spec_ref, held, 288)

    for jj in range(4):
        block = held[pl.ds(4 * step + jj, L, stride=JD), :]
        flipped = jnp.transpose(block).astype(BF16)
        turned[64 * jj : 64 * jj + 64, :L] = flipped[:64]
        turned[64 * jj : 64 * jj + 64, L:] = flipped[64:]
    field = jnp.dot(turned[...], table_ref[...], preferred_element_type=F32)
    out_ref[...] = field.astype(BF16).reshape(4, 64, NLON)


def inverse(spec, table):
    return pl.pallas_call(
        inverse_kernel,
        grid=(JD // 4,),
        in_specs=[
            pl.BlockSpec((OWNERS, 288, 128), lambda s: (0, 0, 0)),
            pl.BlockSpec((2 * L, NLON), lambda s: (0, 0)),
        ],
        out_specs=pl.BlockSpec((4, 64, NLON), lambda s: (s, 0, 0)),
        out_shape=jax.ShapeDtypeStruct((JD, 64, NLON), BF16),
        scratch_shapes=[pltpu.VMEM((L * JD, 128), F32), pltpu.VMEM((256, 2 * L), BF16)],
        compiler_params=params(40),
        cost_estimate=pl.CostEstimate(
            flops=2 * 1536 * 768 * 768, bytes_accessed=6_000_000, transcendentals=0
        ),
        name="inverse_dft",
    )(spec, table)


def exchange(x, axes):
    return lax.all_to_all(x, axes, split_axis=0, concat_axis=0, tiled=True)


def mixing_matrices(gathered):
    w = gathered.reshape(4, 2, 3, 2, 64, 2, 64)
    real, imag = w[:, :, :, 0], w[:, :, :, 1]
    both = jnp.stack(
        [jnp.stack([real, imag], axis=5), jnp.stack([-imag, real], axis=5)], axis=3
    )
    return both.transpose(0, 2, 1, 3, 4, 5, 6, 7).reshape(12, 256, 256)


def shards(inputs, cotangent, weight):
    owner = (lax.axis_index("zh") * 4 + lax.axis_index("y")) * 2 + lax.axis_index("lon")
    lat_rank = lax.axis_index("zh") * 4 + lax.axis_index("y")
    table = jnp.asarray(fourier_rows())
    lat = np.arange(NLAT, dtype=np.float64)
    quad = (2.0 * math.pi * np.sin(math.pi * (lat + 0.5) / NLAT) / math.sqrt(NLAT)).astype(np.float32)
    quad = jnp.asarray(np.broadcast_to(quad[:, None], (NLAT, 128)))
    local_quad = lax.dynamic_slice_in_dim(quad, lat_rank * JD, JD, 0).reshape(JD, 1, 128)

    spec_out = exchange(dft(cotangent[0], table, jnp.ones((JD, 1, 128), F32)), ORDER_AXES)
    spec_in = exchange(dft(inputs[0], table, local_quad), ORDER_AXES)
    gathered = lax.all_gather(weight, ("zh", "lon"), axis=0, tiled=False)
    weights = mixing_matrices(gathered)
    legend = legendre(owner)

    base = 1.0 / math.sqrt(NLAT)
    factor = jnp.full((16, 256), 2.0 * base, F32)
    factor = factor.at[0].set(jnp.where(owner == 0, base, 2.0 * base))
    grads = exchange(analyse(spec_out, legend, factor, "analyse_grad"), DEGREE_AXES)
    mixed = exchange(mix(grads, weights), DEGREE_AXES)
    grid = exchange(synthesise(mixed, legend, quad), ORDER_AXES)
    coeffs = exchange(
        analyse(spec_in, legend, jnp.ones((16, 256), F32), "analyse_field"), DEGREE_AXES
    )
    partial = weight_grads(coeffs, grads)
    weight_grad = lax.psum_scatter(partial, ("zh", "lon"), scatter_dimension=0, tiled=False)
    field = inverse(grid, table)
    return field[None], weight_grad.reshape(3, 2, 64, 128)


def solution(mesh):
    fine = Mesh(mesh.devices.reshape(4, 4, 2, 8), ("zh", "y", "lon", "dp"))
    field = P("dp", ("zh", "y"), "lon", None)
    spectral = P(("zh", "y", "dp"), None, "lon", None)
    return jax.shard_map(
        shards,
        mesh=fine,
        in_specs=(field, field, spectral),
        out_specs=(field, spectral),
        check_vma=False,
    )
```

```python
import math

import jax
import jax.numpy as jnp
import numpy as np
from jax import lax
from jax.experimental import pallas as pl
from jax.experimental.pallas import tpu as pltpu
from jax.sharding import Mesh
from jax.sharding import PartitionSpec as P

L = 384
NLON = 768
NLAT = 384
C = 128
OWNERS = 32
SLOTS = 12
JD = 24
PAIR_ROWS = 96
MIB = 1024 * 1024
F32 = jnp.float32
BF16 = jnp.bfloat16
ORDER_AXES = ("zh", "y", "lon")


def order_of(owner, slot):
    half = slot // 2
    return 64 * half + owner if slot % 2 == 0 else 64 * half + 63 - owner


def pair_index():
    table, count = {}, 0
    for slot in range(SLOTS):
        for group in range(slot // 3, 4):
            for i in range(3):
                table[slot, group, i] = count
                count += 1
    return table


PAIRS = pair_index()


def fourier_rows():
    orders = np.array([order_of(o, k) for o in range(OWNERS) for k in range(SLOTS)], np.int64)
    phase = (orders[:, None] * np.arange(NLON)[None, :] % NLON) * (2.0 * math.pi / NLON)
    rows = np.concatenate([np.cos(phase), -np.sin(phase)], axis=0) / math.sqrt(NLON)
    return rows.astype(np.float32).astype(jnp.bfloat16)


def params(limit):
    return pltpu.CompilerParams(vmem_limit_bytes=limit * MIB)


def vmem_spec():
    return pl.BlockSpec(memory_space=pltpu.VMEM)


def low_half(shape):
    return lax.broadcasted_iota(jnp.int32, shape, len(shape) - 1) < 64


def widen(src_ref, held, rows):
    def body(o, _):
        start = pl.multiple_of(o * rows, rows)
        held[pl.ds(start, rows), :] = src_ref[o].astype(F32)
        return 0

    lax.fori_loop(0, OWNERS, body, 0)


def narrow(held, out_ref, rows):
    def body(o, _):
        start = pl.multiple_of(o * rows, rows)
        out_ref[o] = held[pl.ds(start, rows), :].astype(BF16)
        return 0

    lax.fori_loop(0, OWNERS, body, 0)


def position():
    z = lax.axis_index("zh") * 2 + lax.axis_index("lon")
    return z, lax.axis_index("y"), lax.axis_index("dp")


def place(z, y, dp):
    return (z // 2, y, lax.rem(z, 2), dp)


def transform(step, x_ref, table_ref, scale_ref, out_ref, held):
    x = x_ref[...].reshape(128, NLON)
    spec = lax.dot_general(
        table_ref[...], x, (((1,), (1,)), ((), ())), preferred_element_type=F32
    )
    real, imag = spec[:L], spec[L:]
    low = low_half((L, 128))
    even = jnp.where(low, real, pltpu.roll(imag, 64, 1))
    odd = jnp.where(low, pltpu.roll(real, 64, 1), imag)
    scale = scale_ref[...]
    held[pl.ds(2 * step, L, stride=JD), :] = even * scale[0]
    held[pl.ds(2 * step + 1, L, stride=JD), :] = odd * scale[1]

    @pl.when(step == JD // 2 - 1)
    def _():
        narrow(held, out_ref, 288)


def dft_kernel(x_ref, table_ref, scale_ref, out_ref, held):
    transform(pl.program_id(0), x_ref, table_ref, scale_ref, out_ref, held)


def dft_gather_kernel(
    x_ref, table_ref, scale_ref, weight_ref, out_ref, gathered_ref, held, sent, got, own
):
    step = pl.program_id(0)
    z, y, dp = position()

    def copy(t):
        peer = lax.rem(z + t, 8)
        return pltpu.make_async_remote_copy(
            src_ref=weight_ref,
            dst_ref=gathered_ref.at[z],
            send_sem=sent.at[t],
            recv_sem=got.at[t],
            device_id=place(peer, y, dp),
            device_id_type=pl.DeviceIdType.MESH,
        )

    def keep():
        return pltpu.make_async_copy(weight_ref, gathered_ref.at[z], own)

    @pl.when(step == 0)
    def _():
        barrier = pltpu.get_barrier_semaphore()
        for t in range(1, 8):
            pl.semaphore_signal(
                barrier,
                inc=1,
                device_id=place(lax.rem(z + t, 8), y, dp),
                device_id_type=pl.DeviceIdType.MESH,
            )
        pl.semaphore_wait(barrier, 7)
        for t in range(1, 8):
            copy(t).start()
        keep().start()

    transform(step, x_ref, table_ref, scale_ref, out_ref, held)

    @pl.when(step == JD // 2 - 1)
    def _():
        for t in range(1, 8):
            copy(t).wait()
        keep().wait()


def dft_inputs():
    return [
        pl.BlockSpec((2, 64, NLON), lambda s: (s, 0, 0)),
        pl.BlockSpec((2 * L, NLON), lambda s: (0, 0)),
        pl.BlockSpec((2, 1, 128), lambda s: (s, 0, 0)),
    ]


def dft_cost():
    return pl.CostEstimate(flops=2 * 1536 * 768 * 768, bytes_accessed=6_000_000, transcendentals=0)


def dft(x, table, scale):
    return pl.pallas_call(
        dft_kernel,
        grid=(JD // 2,),
        in_specs=dft_inputs(),
        out_specs=pl.BlockSpec((OWNERS, 288, 128), lambda s: (0, 0, 0)),
        out_shape=jax.ShapeDtypeStruct((OWNERS, 288, 128), BF16),
        scratch_shapes=[pltpu.VMEM((L * JD, 128), F32)],
        compiler_params=params(40),
        cost_estimate=dft_cost(),
        name="dft",
    )(x, table, scale)


def dft_gather(x, table, scale, weight):
    return pl.pallas_call(
        dft_gather_kernel,
        grid=(JD // 2,),
        in_specs=dft_inputs() + [pl.BlockSpec(memory_space=pl.ANY)],
        out_specs=[
            pl.BlockSpec((OWNERS, 288, 128), lambda s: (0, 0, 0)),
            pl.BlockSpec(memory_space=pl.ANY),
        ],
        out_shape=[
            jax.ShapeDtypeStruct((OWNERS, 288, 128), BF16),
            jax.ShapeDtypeStruct((8, L, 128), BF16),
        ],
        scratch_shapes=[
            pltpu.VMEM((L * JD, 128), F32),
            pltpu.SemaphoreType.DMA((8,)),
            pltpu.SemaphoreType.DMA((8,)),
            pltpu.SemaphoreType.DMA,
        ],
        compiler_params=pltpu.CompilerParams(
            vmem_limit_bytes=40 * MIB, collective_id=1, has_side_effects=True
        ),
        cost_estimate=dft_cost(),
        name="dft_gather",
    )(x, table, scale, weight)


def legendre_kernel(order_ref, seed_ref, unscale_ref, cos_ref, up_ref, down_ref, out_ref, held):
    order = order_ref[...]
    cosine = cos_ref[...]

    def advance(degree, row, previous, before):
        up = up_ref[degree]
        down = down_ref[degree]
        fresh = []
        for c in range(3):
            lanes = slice(128 * c, 128 * c + 128)
            value = up * (cosine[:, lanes] * previous[c] - down * before[c])
            value = jnp.where(order == degree, seed_ref[:, lanes], value)
            value = jnp.where(order > degree, 0.0, value)
            held[c, pl.ds(row, 16, stride=L), :] = value * unscale_ref[:, lanes]
            fresh.append(value)
        return fresh, previous

    def body(step, carry):
        previous, before = list(carry[:3]), list(carry[3:])
        group = step // 32
        d = step - 32 * group
        for i in range(3):
            previous, before = advance(3 * step + i, 96 * group + 32 * i + d, previous, before)
        return tuple(previous) + tuple(before)

    zero = jnp.zeros((16, 128), F32)
    lax.fori_loop(0, L // 3, body, (zero,) * 6)

    def convert(k, _):
        start = pl.multiple_of(k * L, L)
        for c in range(3):
            out_ref[pl.ds(start, L), 128 * c : 128 * c + 128] = held[
                c, pl.ds(start, L), :
            ].astype(BF16)
        return 0

    lax.fori_loop(0, SLOTS, convert, 0)


def legendre(owner):
    lat_index = jnp.arange(NLAT, dtype=F32)
    colatitude = math.pi * (lat_index + 0.5) / NLAT
    cosine = jnp.cos(colatitude)[None, :]
    sine_v = jnp.sin(colatitude)[None, :]
    slots = jnp.arange(16, dtype=jnp.int32)
    orders = jnp.where(slots % 2 == 0, 64 * (slots // 2) + owner, 64 * (slots // 2) + 63 - owner)
    orders = jnp.minimum(orders, L - 1)
    step_nums = np.arange(1, L, dtype=np.float64)
    cumlog = np.concatenate([np.zeros(1), np.cumsum(np.log1p(-0.5 / step_nums))]).astype(np.float32)
    selector = (orders[:, None] == jnp.arange(L, dtype=jnp.int32)[None, :]).astype(F32)
    order_log = jnp.sum(selector * cumlog[None, :], axis=1)
    order_f = orders.astype(F32)[:, None]
    log_start = 0.5 * (
        jnp.log(2.0 * order_f + 1.0) - math.log(4.0 * math.pi) + order_log[:, None]
    ) + order_f * jnp.log(sine_v)
    shift_up = jnp.clip(-log_start - 60.0, 0.0, 80.0)
    seed_row = jnp.exp(log_start + shift_up)
    unscale = jnp.exp(-shift_up)
    degree_f = jnp.arange(L, dtype=F32)[:, None]
    order_g = orders.astype(F32)[None, :]
    upward = jnp.sqrt(
        jnp.maximum(4.0 * degree_f * degree_f - 1.0, 1.0)
        / jnp.maximum(degree_f * degree_f - order_g * order_g, 1.0)
    )
    lower = degree_f - 1.0
    backward = jnp.sqrt(
        jnp.maximum(lower * lower - order_g * order_g, 0.0)
        / jnp.maximum(4.0 * lower * lower - 1.0, 1.0)
    )
    wide = (L, 16, 128)
    return pl.pallas_call(
        legendre_kernel,
        in_specs=[vmem_spec()] * 6,
        out_specs=vmem_spec(),
        out_shape=jax.ShapeDtypeStruct((SLOTS * L, NLAT), BF16),
        scratch_shapes=[pltpu.VMEM((3, 16 * L, 128), F32)],
        compiler_params=params(48),
        cost_estimate=pl.CostEstimate(
            flops=10 * 16 * 384 * 384, bytes_accessed=10_000_000, transcendentals=0
        ),
        name="legendre",
    )(
        jnp.broadcast_to(orders[:, None], (16, 128)),
        seed_row,
        unscale,
        jnp.broadcast_to(cosine, (16, NLAT)),
        jnp.broadcast_to(upward[:, :, None], wide),
        jnp.broadcast_to(backward[:, :, None], wide),
    )


def analyse(spec_ref, table_ref, factor_ref, out_ref, field, packed):
    widen(spec_ref, field, 288)
    for k in range(SLOTS):
        first = k // 3
        columns = []
        for lon in range(2):
            pieces = [
                field[(2 * s + lon) * 288 + k * JD : (2 * s + lon) * 288 + k * JD + JD, :]
                for s in range(16)
            ]
            columns.append(jnp.concatenate(pieces, axis=0).astype(BF16))
        data = jnp.concatenate(columns, axis=1)
        rows = table_ref[k * L + 96 * first : (k + 1) * L, :]
        result = jnp.dot(rows, data, preferred_element_type=F32)
        if factor_ref is not None:
            result = result * factor_ref[k : k + 1, :]
        for group in range(first, 4):
            for i in range(3):
                at = ((group - first) * 3 + i) * 32
                for lon in range(2):
                    row = lon * PAIR_ROWS + PAIRS[k, group, i]
                    packed[pl.ds(row, 32, stride=192), :] = result[
                        at : at + 32, 128 * lon : 128 * lon + 128
                    ]
    narrow(packed, out_ref, 192)


def degree_rows(held, group, i):
    parts = []
    for lon in range(2):
        pieces = [
            held[pl.ds(lon * PAIR_ROWS + PAIRS[k, group, i], 32, stride=192), :]
            for k in range(3 * group + 3)
        ]
        parts.append(jnp.concatenate(pieces, axis=0).astype(BF16))
    return jnp.concatenate(parts, axis=1)


def mix(grad_ref, weight_ref, out_ref, held, packed):
    widen(grad_ref, held, 192)
    for group in range(4):
        for i in range(3):
            rows = degree_rows(held, group, i)
            mixed = lax.dot_general(
                rows,
                weight_ref[group * 3 + i],
                (((1,), (1,)), ((), ())),
                preferred_element_type=F32,
            )
            for k in range(3 * group + 3):
                for lon in range(2):
                    row = lon * PAIR_ROWS + PAIRS[k, group, i]
                    packed[pl.ds(row, 32, stride=192), :] = mixed[
                        32 * k : 32 * k + 32, 128 * lon : 128 * lon + 128
                    ]
    narrow(packed, out_ref, 192)


def weight_grads(coeff_ref, grad_ref, out_ref, held_c, held_g):
    widen(coeff_ref, held_c, 192)
    widen(grad_ref, held_g, 192)
    low = low_half((64, 128))
    for group in range(4):
        for i in range(3):
            coeffs = degree_rows(held_c, group, i)
            grads = degree_rows(held_g, group, i)
            product = lax.dot_general(
                coeffs, grads, (((0,), (0,)), ((), ())), preferred_element_type=F32
            ) * 0.125
            for lon in range(2):
                turned = []
                for half in range(2):
                    lanes = slice(128 * half, 128 * half + 128)
                    with_real = product[128 * lon : 128 * lon + 64, lanes]
                    with_imag = pltpu.roll(product[128 * lon + 64 : 128 * lon + 128, lanes], 64, 1)
                    turned.append(jnp.where(low, with_real + with_imag, with_real - with_imag))
                first, second = turned
                out_ref[2 * group + lon, 128 * i : 128 * i + 64, :] = jnp.where(
                    low, first, pltpu.roll(second, 64, 1)
                ).astype(out_ref.dtype)
                out_ref[2 * group + lon, 128 * i + 64 : 128 * i + 128, :] = jnp.where(
                    low, pltpu.roll(first, 64, 1), second
                ).astype(out_ref.dtype)


def synthesise(mixed_ref, table_ref, quad_ref, out_ref, held, grid):
    widen(mixed_ref, held, 192)
    for k in range(SLOTS):
        first = k // 3
        parts = []
        for lon in range(2):
            pieces = [
                held[pl.ds(lon * PAIR_ROWS + PAIRS[k, group, i], 32, stride=192), :]
                for group in range(first, 4)
                for i in range(3)
            ]
            parts.append(jnp.concatenate(pieces, axis=0).astype(BF16))
        data = jnp.concatenate(parts, axis=1)
        rows = table_ref[k * L + 96 * first : (k + 1) * L, :]
        result = lax.dot_general(
            rows, data, (((0,), (0,)), ((), ())), preferred_element_type=F32
        )
        for lon in range(2):
            scaled = result[:, 128 * lon : 128 * lon + 128] * quad_ref[...]
            for s in range(16):
                at = (2 * s + lon) * 288 + k * JD
                grid[at : at + JD, :] = scaled[s * JD : s * JD + JD]
    narrow(grid, out_ref, 288)


def core_kernel(
    spec_ref,
    field_ref,
    table_ref,
    weight_ref,
    factor_ref,
    quad_ref,
    grid_ref,
    partial_ref,
    field_in,
    grid_out,
    degree_out,
    degree_in,
    partial_out,
    wide,
    packed_a,
    packed_b,
    order_sent,
    order_got,
    degree_sent,
    degree_got,
    z_sent,
    z_got,
):
    z, y, dp = position()
    me_order = ((z // 2) * 4 + y) * 2 + lax.rem(z, 2)
    me_degree = y * 8 + dp

    def order_peer(t):
        at = lax.rem(t * 13, 32)
        return lax.rem(z + lax.rem(at, 8), 8), lax.rem(y + at // 8, 4)

    def degree_peer(t):
        at = lax.rem(t * 13, 32)
        return lax.rem(y + lax.rem(at, 4), 4), lax.rem(dp + at // 4, 8)

    def order_copy(n, src, dst, t):
        pz, py = order_peer(t)
        return pltpu.make_async_remote_copy(
            src_ref=src.at[((pz // 2) * 4 + py) * 2 + lax.rem(pz, 2)],
            dst_ref=dst.at[me_order],
            send_sem=order_sent.at[n, t],
            recv_sem=order_got.at[n, t],
            device_id=place(pz, py, dp),
            device_id_type=pl.DeviceIdType.MESH,
        )

    def degree_copy(n, t):
        py, pd = degree_peer(t)
        return pltpu.make_async_remote_copy(
            src_ref=degree_out.at[n, py * 8 + pd],
            dst_ref=degree_in.at[n, me_degree],
            send_sem=degree_sent.at[n, t],
            recv_sem=degree_got.at[n, t],
            device_id=place(z, py, pd),
            device_id_type=pl.DeviceIdType.MESH,
        )

    def z_copy(t):
        pz = lax.rem(z + t, 8)
        return pltpu.make_async_remote_copy(
            src_ref=partial_out.at[pz],
            dst_ref=partial_ref.at[z],
            send_sem=z_sent.at[t],
            recv_sem=z_got.at[t],
            device_id=place(pz, y, dp),
            device_id_type=pl.DeviceIdType.MESH,
        )

    def each(first, end, action):
        def body(t, _):
            action(t)
            return 0

        lax.fori_loop(first, end, body, 0)

    def send_field(first, end):
        each(first, end, lambda t: order_copy(0, field_ref, field_in, t).start())

    def send_grid(first, end):
        each(first, end, lambda t: order_copy(1, grid_out, grid_ref, t).start())

    def send_degrees(n):
        each(1, 32, lambda t: degree_copy(n, t).start())
        degree_in[n, me_degree] = degree_out[n, me_degree]

    def wait_degrees(n):
        each(1, 32, lambda t: degree_copy(n, t).wait())

    barrier = pltpu.get_barrier_semaphore()

    def greet(t):
        pz, py = order_peer(t)
        pl.semaphore_signal(
            barrier, inc=1, device_id=place(pz, py, dp), device_id_type=pl.DeviceIdType.MESH
        )
        py, pd = degree_peer(t)
        pl.semaphore_signal(
            barrier, inc=1, device_id=place(z, py, pd), device_id_type=pl.DeviceIdType.MESH
        )

    each(1, 32, greet)
    pl.semaphore_wait(barrier, 62)

    send_field(1, 9)
    field_in[me_order] = field_ref[me_order]
    packed_a[...] = jnp.zeros_like(packed_a)
    packed_b[...] = jnp.zeros_like(packed_b)
    analyse(spec_ref, table_ref, factor_ref, degree_out.at[0], wide, packed_a)
    send_degrees(0)
    send_field(9, 21)
    wait_degrees(0)
    mix(degree_in.at[0], weight_ref, degree_out.at[1], packed_b, packed_a)
    send_degrees(1)
    send_field(21, 32)
    wait_degrees(1)
    synthesise(degree_in.at[1], table_ref, quad_ref, grid_out, packed_b, wide)
    send_grid(1, 9)
    grid_ref[me_order] = grid_out[me_order]
    each(1, 32, lambda t: order_copy(0, field_ref, field_in, t).wait())
    analyse(field_in, table_ref, None, degree_out.at[2], wide, packed_a)
    send_degrees(2)
    send_grid(9, 20)
    wait_degrees(2)
    send_grid(20, 24)
    weight_grads(degree_in.at[2], degree_in.at[0], partial_out, packed_a, packed_b)
    each(1, 8, lambda t: z_copy(t).start())
    partial_ref[z] = partial_out[z]
    send_grid(24, 32)
    each(1, 8, lambda t: z_copy(t).wait())
    each(1, 32, lambda t: order_copy(1, grid_out, grid_ref, t).wait())


def core(spec, field, table, weights, factor, quad):
    return pl.pallas_call(
        core_kernel,
        in_specs=[vmem_spec()] * 6,
        out_specs=[vmem_spec()] * 2,
        out_shape=[
            jax.ShapeDtypeStruct((OWNERS, 288, 128), BF16),
            jax.ShapeDtypeStruct((8, L, 128), BF16),
        ],
        scratch_shapes=[
            pltpu.VMEM((OWNERS, 288, 128), BF16),
            pltpu.VMEM((OWNERS, 288, 128), BF16),
            pltpu.VMEM((3, OWNERS, 192, 128), BF16),
            pltpu.VMEM((3, OWNERS, 192, 128), BF16),
            pltpu.VMEM((8, L, 128), BF16),
            pltpu.VMEM((OWNERS * 288, 128), F32),
            pltpu.VMEM((OWNERS * 192, 128), F32),
            pltpu.VMEM((OWNERS * 192, 128), F32),
            pltpu.SemaphoreType.DMA((2, 32)),
            pltpu.SemaphoreType.DMA((2, 32)),
            pltpu.SemaphoreType.DMA((3, 32)),
            pltpu.SemaphoreType.DMA((3, 32)),
            pltpu.SemaphoreType.DMA((8,)),
            pltpu.SemaphoreType.DMA((8,)),
        ],
        compiler_params=pltpu.CompilerParams(
            vmem_limit_bytes=58 * MIB, collective_id=2, has_side_effects=True
        ),
        cost_estimate=pl.CostEstimate(
            flops=7_000_000_000, bytes_accessed=16_000_000, transcendentals=0
        ),
        name="core",
    )(spec, field, table, weights, factor, quad)


def inverse_kernel(spec_ref, table_ref, out_ref, held, turned):
    step = pl.program_id(0)

    @pl.when(step == 0)
    def _():
        widen(spec_ref, held, 288)

    for jj in range(4):
        block = held[pl.ds(4 * step + jj, L, stride=JD), :]
        flipped = jnp.transpose(block).astype(BF16)
        turned[64 * jj : 64 * jj + 64, :L] = flipped[:64]
        turned[64 * jj : 64 * jj + 64, L:] = flipped[64:]
    field = jnp.dot(turned[...], table_ref[...], preferred_element_type=F32)
    out_ref[...] = field.astype(BF16).reshape(4, 64, NLON)


def inverse(spec, table):
    return pl.pallas_call(
        inverse_kernel,
        grid=(JD // 4,),
        in_specs=[
            pl.BlockSpec((OWNERS, 288, 128), lambda s: (0, 0, 0)),
            pl.BlockSpec((2 * L, NLON), lambda s: (0, 0)),
        ],
        out_specs=pl.BlockSpec((4, 64, NLON), lambda s: (s, 0, 0)),
        out_shape=jax.ShapeDtypeStruct((JD, 64, NLON), BF16),
        scratch_shapes=[pltpu.VMEM((L * JD, 128), F32), pltpu.VMEM((256, 2 * L), BF16)],
        compiler_params=params(40),
        cost_estimate=pl.CostEstimate(
            flops=2 * 1536 * 768 * 768, bytes_accessed=6_000_000, transcendentals=0
        ),
        name="inverse_dft",
    )(spec, table)


def exchange(x, axes):
    return lax.all_to_all(x, axes, split_axis=0, concat_axis=0, tiled=True)


def mixing_matrices(gathered):
    w = gathered.reshape(4, 2, 3, 2, 64, 2, 64)
    real, imag = w[:, :, :, 0], w[:, :, :, 1]
    both = jnp.stack(
        [jnp.stack([real, imag], axis=5), jnp.stack([-imag, real], axis=5)], axis=3
    )
    return both.transpose(0, 2, 1, 3, 4, 5, 6, 7).reshape(12, 256, 256)


def shards(inputs, cotangent, weight):
    owner = (lax.axis_index("zh") * 4 + lax.axis_index("y")) * 2 + lax.axis_index("lon")
    lat_rank = lax.axis_index("zh") * 4 + lax.axis_index("y")
    table = jnp.asarray(fourier_rows())
    lat = np.arange(NLAT, dtype=np.float64)
    quad = (2.0 * math.pi * np.sin(math.pi * (lat + 0.5) / NLAT) / math.sqrt(NLAT)).astype(np.float32)
    quad = jnp.asarray(np.broadcast_to(quad[:, None], (NLAT, 128)))
    local_quad = lax.dynamic_slice_in_dim(quad, lat_rank * JD, JD, 0).reshape(JD, 1, 128)

    spec_out, gathered = dft_gather(
        cotangent[0], table, jnp.ones((JD, 1, 128), F32), weight.reshape(L, 128)
    )
    spec_out = exchange(spec_out, ORDER_AXES)
    spec_in = dft(inputs[0], table, local_quad)
    weights = mixing_matrices(gathered)
    legend = legendre(owner)
    base = 1.0 / math.sqrt(NLAT)
    factor = jnp.full((16, 256), 2.0 * base, F32)
    factor = factor.at[0].set(jnp.where(owner == 0, base, 2.0 * base))
    grid, partial = core(spec_out, spec_in, legend, weights, factor, quad)
    weight_grad = jnp.sum(partial.astype(F32), axis=0)
    field = inverse(grid, table)
    return field[None], weight_grad.reshape(3, 2, 64, 128)


def solution(mesh):
    fine = Mesh(mesh.devices.reshape(4, 4, 2, 8), ("zh", "y", "lon", "dp"))
    field = P("dp", ("zh", "y"), "lon", None)
    spectral = P(("zh", "y", "dp"), None, "lon", None)
    return jax.shard_map(
        shards,
        mesh=fine,
        in_specs=(field, field, spectral),
        out_specs=(field, spectral),
        check_vma=False,
    )
```

```python
import math

import jax
import jax.numpy as jnp
import numpy as np
from jax import lax
from jax.experimental import pallas as pl
from jax.experimental.pallas import tpu as pltpu
from jax.sharding import Mesh
from jax.sharding import PartitionSpec as P

L = 384
NLON = 768
NLAT = 384
C = 128
OWNERS = 32
SLOTS = 12
JD = 24
MIB = 1024 * 1024
F32 = jnp.float32
BF16 = jnp.bfloat16


def order_of(owner, slot):
    half = slot // 2
    return 64 * half + owner if slot % 2 == 0 else 64 * half + 63 - owner


SETS = (range(0, 4), range(4, SLOTS))
SET_ROWS = 96
HALF_ROWS = 48
ALL_ROWS = 192


def row_index():
    table = {}
    for number, slots in enumerate(SETS):
        count = 0
        for slot in slots:
            for group in range(slot // 3, 4):
                for i in range(3):
                    for lon in range(2):
                        table[slot, group, i, lon] = SET_ROWS * number + HALF_ROWS * lon + count
                    count += 1
    return table


ROWS = row_index()


def fourier_rows():
    orders = np.array([order_of(o, k) for o in range(OWNERS) for k in range(SLOTS)], np.int64)
    phase = (orders[:, None] * np.arange(NLON)[None, :] % NLON) * (2.0 * math.pi / NLON)
    rows = np.concatenate([np.cos(phase), -np.sin(phase)], axis=0) / math.sqrt(NLON)
    return rows.astype(np.float32).astype(jnp.bfloat16)


def legendre_seeds():
    lat = np.arange(NLAT, dtype=np.float64)
    sine = np.sin(math.pi * (lat + 0.5) / NLAT)
    steps = np.arange(1, L, dtype=np.float64)
    cumlog = np.concatenate([np.zeros(1), np.cumsum(np.log1p(-0.5 / steps))])
    orders = np.array(
        [[min(order_of(o, k), L - 1) for k in range(16)] for o in range(OWNERS)], np.int64
    )
    m = orders[:, :, None].astype(np.float64)
    log_start = 0.5 * (
        np.log(2.0 * m + 1.0) - math.log(4.0 * math.pi) + cumlog[orders][:, :, None]
    ) + m * np.log(sine)[None, None, :]
    shift = np.clip(-log_start - 60.0, 0.0, 80.0)
    seed = np.exp(log_start + shift)
    seed = np.where(seed < 1.2e-38, 0.0, seed)
    return seed.astype(np.float32), np.exp(-shift).astype(np.float32)


def low_half(shape):
    return lax.broadcasted_iota(jnp.int32, shape, len(shape) - 1) < 64


def position():
    z = lax.axis_index("zh") * 2 + lax.axis_index("lon")
    return z, lax.axis_index("y"), lax.axis_index("dp")


def place(z, y, dp):
    return (z // 2, y, lax.rem(z, 2), dp)


def widen(src_ref, held, stride, first, rows):
    def body(o, _):
        start = pl.multiple_of(o * stride + first, 16)
        held[pl.ds(start, rows), :] = src_ref[o, first : first + rows, :].astype(F32)
        return 0

    lax.fori_loop(0, OWNERS, body, 0)


def narrow(held, out_ref, stride, first, rows):
    def body(o, _):
        start = pl.multiple_of(o * stride + first, 16)
        out_ref[o, first : first + rows, :] = held[pl.ds(start, rows), :].astype(BF16)
        return 0

    lax.fori_loop(0, OWNERS, body, 0)


def transform(x_ref, fourier_ref, out_ref, held, scale_of):
    low = low_half((L, 128))

    def body(step, _):
        x = x_ref[pl.ds(2 * step, 2)].reshape(128, NLON)
        spec = lax.dot_general(
            fourier_ref[...], x, (((1,), (1,)), ((), ())), preferred_element_type=F32
        )
        real, imag = spec[:L], spec[L:]
        even = jnp.where(low, real, pltpu.roll(imag, 64, 1))
        odd = jnp.where(low, pltpu.roll(real, 64, 1), imag)
        if scale_of is not None:
            even = even * scale_of(2 * step)
            odd = odd * scale_of(2 * step + 1)
        held[pl.ds(2 * step, L, stride=JD), :] = even
        held[pl.ds(2 * step + 1, L, stride=JD), :] = odd
        return 0

    lax.fori_loop(0, JD // 2, body, 0)
    narrow(held, out_ref, 288, 0, 288)


def legendre(owner, seed_ref, unscale_ref, cos_ref, out_ref, pool):
    slot = lax.broadcasted_iota(jnp.int32, (16, 128), 0)
    half = 64 * (slot // 2)
    order = jnp.where(lax.rem(slot, 2) == 0, half + owner, half + 63 - owner)
    order = jnp.minimum(order, L - 1)
    order_f = order.astype(F32)
    square = order_f * order_f
    cosine = cos_ref[...]

    def advance(degree, row, previous, before):
        degree_f = jnp.full((16, 128), degree, jnp.int32).astype(F32)
        up = jnp.sqrt(
            jnp.maximum(4.0 * degree_f * degree_f - 1.0, 1.0)
            / jnp.maximum(degree_f * degree_f - square, 1.0)
        )
        lower = degree_f - 1.0
        down = jnp.sqrt(
            jnp.maximum(lower * lower - square, 0.0)
            / jnp.maximum(4.0 * lower * lower - 1.0, 1.0)
        )
        fresh = []
        for c in range(3):
            lanes = slice(128 * c, 128 * c + 128)
            value = up * (cosine[:, lanes] * previous[c] - down * before[c])
            value = jnp.where(order == degree, seed_ref[:, lanes], value)
            value = jnp.where(order > degree, 0.0, value)
            pool[pl.ds(16 * L * c + row, 16, stride=L), :] = value * unscale_ref[:, lanes]
            fresh.append(value)
        return fresh, previous

    def body(step, carry):
        previous, before = list(carry[:3]), list(carry[3:])
        group = step // 32
        d = step - 32 * group
        for i in range(3):
            previous, before = advance(3 * step + i, 96 * group + 32 * i + d, previous, before)
        return tuple(previous) + tuple(before)

    zero = jnp.zeros((16, 128), F32)
    lax.fori_loop(0, L // 3, body, (zero,) * 6)

    def convert(k, _):
        start = pl.multiple_of(k * L, L)
        for c in range(3):
            out_ref[pl.ds(start, L), 128 * c : 128 * c + 128] = pool[
                pl.ds(16 * L * c + start, L), :
            ].astype(BF16)
        return 0

    lax.fori_loop(0, SLOTS, convert, 0)


def mixing_matrices(gathered_ref, out_ref):
    low = low_half((64, 128))
    for group in range(4):
        for i in range(3):
            for lon in range(2):
                source = gathered_ref[2 * group + lon, 128 * i : 128 * i + 128, :].astype(F32)
                real, imag = source[:64], source[64:]
                real_t, imag_t = pltpu.roll(real, 64, 1), pltpu.roll(imag, 64, 1)
                n, at = group * 3 + i, 128 * lon
                out_ref[n, at : at + 64, :128] = jnp.where(low, real, imag_t).astype(BF16)
                out_ref[n, at : at + 64, 128:] = jnp.where(low, real_t, imag).astype(BF16)
                out_ref[n, at + 64 : at + 128, :128] = jnp.where(low, -imag, real_t).astype(BF16)
                out_ref[n, at + 64 : at + 128, 128:] = jnp.where(low, -imag_t, real).astype(BF16)


def analyse(number, field, table_ref, factor_of, out_ref, packed):
    for k in SETS[number]:
        first = k // 3
        columns = []
        for lon in range(2):
            pieces = [
                field[(2 * s + lon) * 288 + k * JD : (2 * s + lon) * 288 + k * JD + JD, :]
                for s in range(16)
            ]
            columns.append(jnp.concatenate(pieces, axis=0).astype(BF16))
        data = jnp.concatenate(columns, axis=1)
        rows = table_ref[k * L + 96 * first : (k + 1) * L, :]
        result = jnp.dot(rows, data, preferred_element_type=F32)
        if factor_of is not None:
            result = result * factor_of(k)
        for group in range(first, 4):
            for i in range(3):
                at = ((group - first) * 3 + i) * 32
                for lon in range(2):
                    packed[pl.ds(ROWS[k, group, i, lon], 32, stride=ALL_ROWS), :] = result[
                        at : at + 32, 128 * lon : 128 * lon + 128
                    ]
    narrow(packed, out_ref, ALL_ROWS, SET_ROWS * number, SET_ROWS)


def degree_rows(held, slots, group, i):
    parts = []
    for lon in range(2):
        pieces = [held[pl.ds(ROWS[k, group, i, lon], 32, stride=ALL_ROWS), :] for k in slots]
        parts.append(jnp.concatenate(pieces, axis=0).astype(BF16))
    return jnp.concatenate(parts, axis=1)


def mix(number, grad_ref, matrix_ref, out_ref, held, packed):
    widen(grad_ref, held, ALL_ROWS, SET_ROWS * number, SET_ROWS)
    for group in range(4):
        slots = [k for k in SETS[number] if k // 3 <= group]
        if not slots:
            continue
        for i in range(3):
            mixed = lax.dot_general(
                degree_rows(held, slots, group, i),
                matrix_ref[group * 3 + i],
                (((1,), (1,)), ((), ())),
                preferred_element_type=F32,
            )
            for n, k in enumerate(slots):
                for lon in range(2):
                    packed[pl.ds(ROWS[k, group, i, lon], 32, stride=ALL_ROWS), :] = mixed[
                        32 * n : 32 * n + 32, 128 * lon : 128 * lon + 128
                    ]
    narrow(packed, out_ref, ALL_ROWS, SET_ROWS * number, SET_ROWS)


def weight_grads(held_c, held_g, out_ref):
    low = low_half((64, 128))
    for group in range(4):
        for i in range(3):
            slots = range(3 * group + 3)
            product = lax.dot_general(
                degree_rows(held_c, slots, group, i),
                degree_rows(held_g, slots, group, i),
                (((0,), (0,)), ((), ())),
                preferred_element_type=F32,
            ) * 0.125
            for lon in range(2):
                turned = []
                for half in range(2):
                    lanes = slice(128 * half, 128 * half + 128)
                    with_real = product[128 * lon : 128 * lon + 64, lanes]
                    with_imag = pltpu.roll(product[128 * lon + 64 : 128 * lon + 128, lanes], 64, 1)
                    turned.append(jnp.where(low, with_real + with_imag, with_real - with_imag))
                first, second = turned
                out_ref[2 * group + lon, 128 * i : 128 * i + 64, :] = jnp.where(
                    low, first, pltpu.roll(second, 64, 1)
                ).astype(BF16)
                out_ref[2 * group + lon, 128 * i + 64 : 128 * i + 128, :] = jnp.where(
                    low, pltpu.roll(first, 64, 1), second
                ).astype(BF16)


def synthesise(number, mixed_ref, table_ref, quad_ref, out_ref, held, grid):
    widen(mixed_ref, held, ALL_ROWS, SET_ROWS * number, SET_ROWS)
    for k in SETS[number]:
        first = k // 3
        parts = []
        for lon in range(2):
            pieces = [
                held[pl.ds(ROWS[k, group, i, lon], 32, stride=ALL_ROWS), :]
                for group in range(first, 4)
                for i in range(3)
            ]
            parts.append(jnp.concatenate(pieces, axis=0).astype(BF16))
        data = jnp.concatenate(parts, axis=1)
        rows = table_ref[k * L + 96 * first : (k + 1) * L, :]
        result = lax.dot_general(
            rows, data, (((0,), (0,)), ((), ())), preferred_element_type=F32
        )
        for lon in range(2):
            scaled = result[:, 128 * lon : 128 * lon + 128] * quad_ref[...]
            for s in range(16):
                at = (2 * s + lon) * 288 + k * JD
                grid[at : at + JD, :] = scaled[s * JD : s * JD + JD]
    slots = SETS[number]
    narrow(grid, out_ref, 288, slots[0] * JD, len(slots) * JD)


def inverse(spec_ref, fourier_ref, out_ref, held, turned):
    widen(spec_ref, held, 288, 0, 288)

    def body(step, _):
        for jj in range(4):
            block = held[pl.ds(4 * step + jj, L, stride=JD), :]
            flipped = jnp.transpose(block).astype(BF16)
            turned[64 * jj : 64 * jj + 64, :L] = flipped[:64]
            turned[64 * jj : 64 * jj + 64, L:] = flipped[64:]
        field = jnp.dot(turned[...], fourier_ref[...], preferred_element_type=F32)
        out_ref[pl.ds(4 * step, 4)] = field.astype(BF16).reshape(4, 64, NLON)
        return 0

    lax.fori_loop(0, JD // 4, body, 0)


def kernel(
    inputs_hbm,
    cotangent_hbm,
    weight_hbm,
    fourier_hbm,
    seed_hbm,
    unscale_hbm,
    cos_hbm,
    quad_hbm,
    field_ref,
    weight_grad_ref,
    inputs_ref,
    cotangent_ref,
    weight_ref,
    fourier_ref,
    seed_ref,
    unscale_ref,
    cos_ref,
    quad_ref,
    table_ref,
    gathered,
    matrices,
    near_out,
    near_in,
    field_out,
    field_in,
    grid_in,
    degree_out,
    degree_in,
    partial_out,
    partial_in,
    turned,
    pool,
    loaded,
    order_sent,
    order_got,
    degree_sent,
    degree_got,
    z_sent,
    z_got,
):
    z, y, dp = position()
    lat_rank = (z // 2) * 4 + y
    me_order = lat_rank * 2 + lax.rem(z, 2)
    me_degree = y * 8 + dp
    mesh_ids = pl.DeviceIdType.MESH
    wide = pool.at[pl.ds(0, OWNERS * 288)]
    packed_a = pool.at[pl.ds(OWNERS * 288, OWNERS * ALL_ROWS)]
    packed_b = pool.at[pl.ds(OWNERS * (288 + ALL_ROWS), OWNERS * ALL_ROWS)]
    order_rows = [(slots[0] * JD, len(slots) * JD) for slots in SETS]

    loads = [
        (cotangent_hbm, cotangent_ref),
        (fourier_hbm, fourier_ref),
        (weight_hbm, weight_ref),
        (inputs_hbm, inputs_ref),
        (seed_hbm.at[me_order], seed_ref),
        (unscale_hbm.at[me_order], unscale_ref),
        (cos_hbm, cos_ref),
        (quad_hbm, quad_ref),
    ]
    loads = [pltpu.make_async_copy(a, b, loaded.at[n]) for n, (a, b) in enumerate(loads)]

    def order_peer(t):
        at = lax.rem(t * 13, 32)
        return lax.rem(z + lax.rem(at, 8), 8), lax.rem(y + at // 8, 4)

    def degree_peer(t):
        at = lax.rem(t * 13, 32)
        return lax.rem(y + lax.rem(at, 4), 4), lax.rem(dp + at // 4, 8)

    def order_copy(n, src, dst, t, first=0, rows=288):
        pz, py = order_peer(t)
        return pltpu.make_async_remote_copy(
            src_ref=src.at[((pz // 2) * 4 + py) * 2 + lax.rem(pz, 2), pl.ds(first, rows)],
            dst_ref=dst.at[me_order, pl.ds(first, rows)],
            send_sem=order_sent.at[n, t],
            recv_sem=order_got.at[n, t],
            device_id=place(pz, py, dp),
            device_id_type=mesh_ids,
        )

    def cotangent_copy(t):
        return order_copy(0, near_out, near_in, t)

    def field_copy(t):
        return order_copy(1, field_out, field_in, t)

    def grid_copy(number, t):
        return order_copy(2 + number, near_out, grid_in, t, *order_rows[number])

    def degree_copy(n, number, t):
        py, pd = degree_peer(t)
        return pltpu.make_async_remote_copy(
            src_ref=degree_out.at[n, py * 8 + pd, pl.ds(SET_ROWS * number, SET_ROWS)],
            dst_ref=degree_in.at[n, me_degree, pl.ds(SET_ROWS * number, SET_ROWS)],
            send_sem=degree_sent.at[2 * n + number, t],
            recv_sem=degree_got.at[2 * n + number, t],
            device_id=place(z, py, pd),
            device_id_type=mesh_ids,
        )

    def weight_copy(t):
        return pltpu.make_async_remote_copy(
            src_ref=weight_ref,
            dst_ref=gathered.at[z],
            send_sem=z_sent.at[0, t],
            recv_sem=z_got.at[0, t],
            device_id=place(lax.rem(z + t, 8), y, dp),
            device_id_type=mesh_ids,
        )

    def partial_copy(t):
        pz = lax.rem(z + t, 8)
        return pltpu.make_async_remote_copy(
            src_ref=partial_out.at[pz],
            dst_ref=partial_in.at[z],
            send_sem=z_sent.at[1, t],
            recv_sem=z_got.at[1, t],
            device_id=place(pz, y, dp),
            device_id_type=mesh_ids,
        )

    def each(first, end, action):
        def body(t, _):
            action(t)
            return 0

        lax.fori_loop(first, end, body, 0)

    def send_field(first, end):
        each(first, end, lambda t: field_copy(t).start())

    def send_grid(number, first, end):
        each(first, end, lambda t: grid_copy(number, t).start())

    def send_degrees(n, number):
        each(1, 32, lambda t: degree_copy(n, number, t).start())
        rows = slice(SET_ROWS * number, SET_ROWS * number + SET_ROWS)
        degree_in[n, me_degree, rows, :] = degree_out[n, me_degree, rows, :]

    def wait_degrees(n, number):
        each(1, 32, lambda t: degree_copy(n, number, t).wait())

    def keep_grid(number):
        first, rows = order_rows[number]
        grid_in[me_order, first : first + rows, :] = near_out[me_order, first : first + rows, :]

    def factor_of(k):
        base = 1.0 / math.sqrt(NLAT)
        return jnp.where(me_order == 0, base, 2.0 * base) if k == 0 else 2.0 * base

    for load in loads:
        load.start()
    barrier = pltpu.get_barrier_semaphore()

    def greet(t):
        pz, py = order_peer(t)
        pl.semaphore_signal(barrier, inc=1, device_id=place(pz, py, dp), device_id_type=mesh_ids)
        py, pd = degree_peer(t)
        pl.semaphore_signal(barrier, inc=1, device_id=place(z, py, pd), device_id_type=mesh_ids)

    each(1, 32, greet)
    loads[2].wait()
    pl.semaphore_wait(barrier, 62)
    each(1, 8, lambda t: weight_copy(t).start())
    gathered[z] = weight_ref[...]
    loads[0].wait()
    loads[1].wait()

    transform(cotangent_ref, fourier_ref, near_out, wide, None)
    each(1, 32, lambda t: cotangent_copy(t).start())
    near_in[me_order] = near_out[me_order]
    for load in loads[3:]:
        load.wait()
    legendre(me_order, seed_ref, unscale_ref, cos_ref, table_ref, pool)
    transform(
        inputs_ref,
        fourier_ref,
        field_out,
        wide,
        lambda j: quad_ref[pl.ds(lat_rank * JD + j, 1), :],
    )
    field_in[me_order] = field_out[me_order]
    each(1, 8, lambda t: weight_copy(t).wait())
    mixing_matrices(gathered, matrices)
    packed_a[...] = jnp.zeros((OWNERS * ALL_ROWS, 128), F32)
    packed_b[...] = jnp.zeros((OWNERS * ALL_ROWS, 128), F32)
    each(1, 32, lambda t: cotangent_copy(t).wait())

    send_field(1, 7)
    widen(near_in, wide, 288, 0, 288)
    analyse(0, wide, table_ref, factor_of, degree_out.at[0], packed_a)
    send_degrees(0, 0)
    send_field(7, 11)
    analyse(1, wide, table_ref, factor_of, degree_out.at[0], packed_a)
    send_degrees(0, 1)
    send_field(11, 17)
    wait_degrees(0, 0)
    mix(0, degree_in.at[0], matrices, degree_out.at[1], packed_b, packed_a)
    send_degrees(1, 0)
    send_field(17, 24)
    wait_degrees(0, 1)
    mix(1, degree_in.at[0], matrices, degree_out.at[1], packed_b, packed_a)
    send_degrees(1, 1)
    send_field(24, 32)
    wait_degrees(1, 0)
    synthesise(0, degree_in.at[1], table_ref, quad_ref, near_out, packed_b, wide)
    send_grid(0, 1, 32)
    keep_grid(0)
    wait_degrees(1, 1)
    synthesise(1, degree_in.at[1], table_ref, quad_ref, near_out, packed_b, wide)
    send_grid(1, 1, 9)
    keep_grid(1)

    each(1, 32, lambda t: field_copy(t).wait())
    widen(field_in, wide, 288, 0, 288)
    analyse(0, wide, table_ref, None, degree_out.at[2], packed_a)
    send_degrees(2, 0)
    analyse(1, wide, table_ref, None, degree_out.at[2], packed_a)
    send_degrees(2, 1)
    send_grid(1, 9, 32)
    widen(degree_in.at[0], packed_b, ALL_ROWS, 0, ALL_ROWS)
    wait_degrees(2, 0)
    wait_degrees(2, 1)
    widen(degree_in.at[2], packed_a, ALL_ROWS, 0, ALL_ROWS)
    weight_grads(packed_a, packed_b, partial_out)
    each(1, 8, lambda t: partial_copy(t).start())
    partial_in[z] = partial_out[z]
    each(1, 32, lambda t: grid_copy(0, t).wait())
    each(1, 32, lambda t: grid_copy(1, t).wait())
    inverse(grid_in, fourier_ref, field_ref, wide, turned)
    each(1, 8, lambda t: partial_copy(t).wait())
    total = partial_in[0].astype(F32)
    for n in range(1, 8):
        total = total + partial_in[n].astype(F32)
    weight_grad_ref[...] = total


def shards(inputs, cotangent, weight):
    seed, unscale = legendre_seeds()
    lat = np.arange(NLAT, dtype=np.float64)
    angle = math.pi * (lat + 0.5) / NLAT
    quad = (2.0 * math.pi * np.sin(angle) / math.sqrt(NLAT)).astype(np.float32)
    quad = np.broadcast_to(quad[:, None], (NLAT, 128))
    cosine = np.broadcast_to(np.cos(angle).astype(np.float32)[None, :], (16, NLAT))
    vmem = pl.BlockSpec(memory_space=pltpu.VMEM)
    anywhere = pl.BlockSpec(memory_space=pl.ANY)
    chunks = pltpu.VMEM((OWNERS, 288, 128), BF16)
    degrees = pltpu.VMEM((3, OWNERS, ALL_ROWS, 128), BF16)
    dma = pltpu.SemaphoreType.DMA
    field, weight_grad = pl.pallas_call(
        kernel,
        in_specs=[anywhere] * 8,
        out_specs=[vmem, vmem],
        out_shape=[
            jax.ShapeDtypeStruct((JD, 64, NLON), BF16),
            jax.ShapeDtypeStruct((L, 128), F32),
        ],
        scratch_shapes=[
            pltpu.VMEM((JD, 64, NLON), BF16),
            pltpu.VMEM((JD, 64, NLON), BF16),
            pltpu.VMEM((L, 128), BF16),
            pltpu.VMEM((2 * L, NLON), BF16),
            pltpu.VMEM((16, NLAT), F32),
            pltpu.VMEM((16, NLAT), F32),
            pltpu.VMEM((16, NLAT), F32),
            pltpu.VMEM((NLAT, 128), F32),
            pltpu.VMEM((SLOTS * L, NLAT), BF16),
            pltpu.VMEM((8, L, 128), BF16),
            pltpu.VMEM((12, 256, 256), BF16),
            chunks,
            chunks,
            chunks,
            chunks,
            chunks,
            degrees,
            degrees,
            pltpu.VMEM((8, L, 128), BF16),
            pltpu.VMEM((8, L, 128), BF16),
            pltpu.VMEM((256, 2 * L), BF16),
            pltpu.VMEM((OWNERS * (288 + 2 * ALL_ROWS), 128), F32),
            dma((8,)),
            dma((4, 32)),
            dma((4, 32)),
            dma((6, 32)),
            dma((6, 32)),
            dma((2, 8)),
            dma((2, 8)),
        ],
        compiler_params=pltpu.CompilerParams(
            vmem_limit_bytes=60 * MIB, collective_id=1, has_side_effects=True
        ),
        cost_estimate=pl.CostEstimate(
            flops=13_000_000_000, bytes_accessed=16_000_000, transcendentals=0
        ),
        name="sphere",
    )(
        inputs[0],
        cotangent[0],
        weight.reshape(L, 128),
        jnp.asarray(fourier_rows()),
        jnp.asarray(seed),
        jnp.asarray(unscale),
        jnp.asarray(cosine),
        jnp.asarray(quad),
    )
    return field[None], weight_grad.reshape(3, 2, 64, 128)


def solution(mesh):
    fine = Mesh(mesh.devices.reshape(4, 4, 2, 8), ("zh", "y", "lon", "dp"))
    field = P("dp", ("zh", "y"), "lon", None)
    spectral = P(("zh", "y", "dp"), None, "lon", None)
    return jax.shard_map(
        shards,
        mesh=fine,
        in_specs=(field, field, spectral),
        out_specs=(field, spectral),
        check_vma=False,
    )
```

```python
import math

import jax
import jax.numpy as jnp
import numpy as np
from jax import lax
from jax.experimental import pallas as pl
from jax.experimental.pallas import tpu as pltpu
from jax.sharding import Mesh
from jax.sharding import PartitionSpec as P

L = 384
NLON = 768
NLAT = 384
C = 128
OWNERS = 32
SLOTS = 12
JD = 24
MIB = 1024 * 1024
F32 = jnp.float32
BF16 = jnp.bfloat16


def order_of(owner, slot):
    half = slot // 2
    return 64 * half + owner if slot % 2 == 0 else 64 * half + 63 - owner


SETS = (range(0, 4), range(4, SLOTS))
SET_ROWS = 96
FIELD_SENT = (31, 31, 31, 31, 31)
GRID_SENT = (8, 8, 31)
HALF_ROWS = 48
ALL_ROWS = 192


def row_index():
    table = {}
    for number, slots in enumerate(SETS):
        count = 0
        for slot in slots:
            for group in range(slot // 3, 4):
                for i in range(3):
                    for lon in range(2):
                        table[slot, group, i, lon] = SET_ROWS * number + HALF_ROWS * lon + count
                    count += 1
    return table


ROWS = row_index()


def fourier_rows():
    orders = np.array([order_of(o, k) for o in range(OWNERS) for k in range(SLOTS)], np.int64)
    phase = (orders[:, None] * np.arange(NLON)[None, :] % NLON) * (2.0 * math.pi / NLON)
    rows = np.concatenate([np.cos(phase), -np.sin(phase)], axis=0) / math.sqrt(NLON)
    return rows.astype(np.float32).astype(jnp.bfloat16)


def legendre_seeds():
    lat = np.arange(NLAT, dtype=np.float64)
    sine = np.sin(math.pi * (lat + 0.5) / NLAT)
    steps = np.arange(1, L, dtype=np.float64)
    cumlog = np.concatenate([np.zeros(1), np.cumsum(np.log1p(-0.5 / steps))])
    orders = np.array(
        [[min(order_of(o, k), L - 1) for k in range(16)] for o in range(OWNERS)], np.int64
    )
    m = orders[:, :, None].astype(np.float64)
    log_start = 0.5 * (
        np.log(2.0 * m + 1.0) - math.log(4.0 * math.pi) + cumlog[orders][:, :, None]
    ) + m * np.log(sine)[None, None, :]
    shift = np.clip(-log_start - 60.0, 0.0, 80.0)
    seed = np.exp(log_start + shift)
    seed = np.where(seed < 1.2e-38, 0.0, seed)
    return np.concatenate([seed, np.exp(-shift)], axis=1).astype(np.float32).reshape(-1, NLAT)


def low_half(shape):
    return lax.broadcasted_iota(jnp.int32, shape, len(shape) - 1) < 64


def position():
    z = lax.axis_index("zh") * 2 + lax.axis_index("lon")
    return z, lax.axis_index("y"), lax.axis_index("dp")


def place(z, y, dp):
    return (z // 2, y, lax.rem(z, 2), dp)


def widen(src_ref, held, stride, first, rows):
    def body(o, _):
        start = pl.multiple_of(o * stride + first, 16)
        held[pl.ds(start, rows), :] = src_ref[o, first : first + rows, :].astype(F32)
        return 0

    lax.fori_loop(0, OWNERS, body, 0)


def narrow(held, out_ref, stride, first, rows):
    def body(o, _):
        start = pl.multiple_of(o * stride + first, 16)
        out_ref[o, first : first + rows, :] = held[pl.ds(start, rows), :].astype(BF16)
        return 0

    lax.fori_loop(0, OWNERS, body, 0)


def transform(x_ref, fourier_ref, held, scale_of, first, end):
    low = low_half((L, 128))

    def body(step, _):
        x = x_ref[pl.ds(2 * step, 2)].reshape(128, NLON)
        spec = lax.dot_general(
            fourier_ref[...], x, (((1,), (1,)), ((), ())), preferred_element_type=F32
        )
        real, imag = spec[:L], spec[L:]
        even = jnp.where(low, real, pltpu.roll(imag, 64, 1))
        odd = jnp.where(low, pltpu.roll(real, 64, 1), imag)
        if scale_of is not None:
            even = even * scale_of(2 * step)
            odd = odd * scale_of(2 * step + 1)
        held[pl.ds(2 * step, L, stride=JD), :] = even
        held[pl.ds(2 * step + 1, L, stride=JD), :] = odd
        return 0

    lax.fori_loop(first, end, body, 0)


def legendre(owner, seed_ref, unscale_ref, cos_ref, out_ref, pool):
    slot = lax.broadcasted_iota(jnp.int32, (16, 128), 0)
    half = 64 * (slot // 2)
    order = jnp.where(lax.rem(slot, 2) == 0, half + owner, half + 63 - owner)
    order = jnp.minimum(order, L - 1)
    order_f = order.astype(F32)
    square = order_f * order_f
    cosine = cos_ref[...]

    def advance(degree, row, previous, before):
        degree_f = jnp.full((16, 128), degree, jnp.int32).astype(F32)
        up = jnp.sqrt(
            jnp.maximum(4.0 * degree_f * degree_f - 1.0, 1.0)
            / jnp.maximum(degree_f * degree_f - square, 1.0)
        )
        lower = degree_f - 1.0
        down = jnp.sqrt(
            jnp.maximum(lower * lower - square, 0.0)
            / jnp.maximum(4.0 * lower * lower - 1.0, 1.0)
        )
        fresh = []
        for c in range(3):
            lanes = slice(128 * c, 128 * c + 128)
            value = up * (cosine[:, lanes] * previous[c] - down * before[c])
            value = jnp.where(order == degree, seed_ref[:, lanes], value)
            value = jnp.where(order > degree, 0.0, value)
            pool[pl.ds(16 * L * c + row, 16, stride=L), :] = value * unscale_ref[:, lanes]
            fresh.append(value)
        return fresh, previous

    def body(step, carry):
        previous, before = list(carry[:3]), list(carry[3:])
        group = step // 32
        d = step - 32 * group
        for i in range(3):
            previous, before = advance(3 * step + i, 96 * group + 32 * i + d, previous, before)
        return tuple(previous) + tuple(before)

    zero = jnp.zeros((16, 128), F32)
    lax.fori_loop(0, L // 3, body, (zero,) * 6)

    def convert(k, _):
        start = pl.multiple_of(k * L, L)
        for c in range(3):
            out_ref[pl.ds(start, L), 128 * c : 128 * c + 128] = pool[
                pl.ds(16 * L * c + start, L), :
            ].astype(BF16)
        return 0

    lax.fori_loop(0, SLOTS, convert, 0)


def mixing_matrices(gathered_ref, out_ref):
    low = low_half((64, 128))
    for group in range(4):
        for i in range(3):
            for lon in range(2):
                source = gathered_ref[2 * group + lon, 128 * i : 128 * i + 128, :].astype(F32)
                real, imag = source[:64], source[64:]
                real_t, imag_t = pltpu.roll(real, 64, 1), pltpu.roll(imag, 64, 1)
                n, at = group * 3 + i, 128 * lon
                out_ref[n, at : at + 64, :128] = jnp.where(low, real, imag_t).astype(BF16)
                out_ref[n, at : at + 64, 128:] = jnp.where(low, real_t, imag).astype(BF16)
                out_ref[n, at + 64 : at + 128, :128] = jnp.where(low, -imag, real_t).astype(BF16)
                out_ref[n, at + 64 : at + 128, 128:] = jnp.where(low, -imag_t, real).astype(BF16)


def analyse(number, field, table_ref, factor_of, out_ref, packed):
    for k in SETS[number]:
        first = k // 3
        columns = []
        for lon in range(2):
            pieces = [
                field[(2 * s + lon) * 288 + k * JD : (2 * s + lon) * 288 + k * JD + JD, :]
                for s in range(16)
            ]
            columns.append(jnp.concatenate(pieces, axis=0).astype(BF16))
        data = jnp.concatenate(columns, axis=1)
        rows = table_ref[k * L + 96 * first : (k + 1) * L, :]
        result = jnp.dot(rows, data, preferred_element_type=F32)
        if factor_of is not None:
            result = result * factor_of(k)
        for group in range(first, 4):
            for i in range(3):
                at = ((group - first) * 3 + i) * 32
                for lon in range(2):
                    packed[pl.ds(ROWS[k, group, i, lon], 32, stride=ALL_ROWS), :] = result[
                        at : at + 32, 128 * lon : 128 * lon + 128
                    ]
    narrow(packed, out_ref, ALL_ROWS, SET_ROWS * number, SET_ROWS)


def degree_rows(held, slots, group, i):
    parts = []
    for lon in range(2):
        pieces = [held[pl.ds(ROWS[k, group, i, lon], 32, stride=ALL_ROWS), :] for k in slots]
        parts.append(jnp.concatenate(pieces, axis=0).astype(BF16))
    return jnp.concatenate(parts, axis=1)


def mix(number, grad_ref, matrix_ref, out_ref, held, packed):
    widen(grad_ref, held, ALL_ROWS, SET_ROWS * number, SET_ROWS)
    for group in range(4):
        slots = [k for k in SETS[number] if k // 3 <= group]
        if not slots:
            continue
        for i in range(3):
            mixed = lax.dot_general(
                degree_rows(held, slots, group, i),
                matrix_ref[group * 3 + i],
                (((1,), (1,)), ((), ())),
                preferred_element_type=F32,
            )
            for n, k in enumerate(slots):
                for lon in range(2):
                    packed[pl.ds(ROWS[k, group, i, lon], 32, stride=ALL_ROWS), :] = mixed[
                        32 * n : 32 * n + 32, 128 * lon : 128 * lon + 128
                    ]
    narrow(packed, out_ref, ALL_ROWS, SET_ROWS * number, SET_ROWS)


def weight_grads(held_c, held_g, out_ref):
    low = low_half((64, 128))
    for group in range(4):
        for i in range(3):
            slots = range(3 * group + 3)
            product = lax.dot_general(
                degree_rows(held_c, slots, group, i),
                degree_rows(held_g, slots, group, i),
                (((0,), (0,)), ((), ())),
                preferred_element_type=F32,
            ) * 0.125
            for lon in range(2):
                turned = []
                for half in range(2):
                    lanes = slice(128 * half, 128 * half + 128)
                    with_real = product[128 * lon : 128 * lon + 64, lanes]
                    with_imag = pltpu.roll(product[128 * lon + 64 : 128 * lon + 128, lanes], 64, 1)
                    turned.append(jnp.where(low, with_real + with_imag, with_real - with_imag))
                first, second = turned
                out_ref[2 * group + lon, 128 * i : 128 * i + 64, :] = jnp.where(
                    low, first, pltpu.roll(second, 64, 1)
                ).astype(BF16)
                out_ref[2 * group + lon, 128 * i + 64 : 128 * i + 128, :] = jnp.where(
                    low, pltpu.roll(first, 64, 1), second
                ).astype(BF16)


def synthesise(number, mixed_ref, table_ref, quad_ref, out_ref, held, grid):
    widen(mixed_ref, held, ALL_ROWS, SET_ROWS * number, SET_ROWS)
    for k in SETS[number]:
        first = k // 3
        parts = []
        for lon in range(2):
            pieces = [
                held[pl.ds(ROWS[k, group, i, lon], 32, stride=ALL_ROWS), :]
                for group in range(first, 4)
                for i in range(3)
            ]
            parts.append(jnp.concatenate(pieces, axis=0).astype(BF16))
        data = jnp.concatenate(parts, axis=1)
        rows = table_ref[k * L + 96 * first : (k + 1) * L, :]
        result = lax.dot_general(
            rows, data, (((0,), (0,)), ((), ())), preferred_element_type=F32
        )
        for lon in range(2):
            scaled = result[:, 128 * lon : 128 * lon + 128] * quad_ref[...]
            for s in range(16):
                at = (2 * s + lon) * 288 + k * JD
                grid[at : at + JD, :] = scaled[s * JD : s * JD + JD]
    slots = SETS[number]
    narrow(grid, out_ref, 288, slots[0] * JD, len(slots) * JD)


def inverse(spec_ref, fourier_ref, out_ref, held, turned):
    widen(spec_ref, held, 288, 0, 288)

    def body(step, _):
        for jj in range(4):
            block = held[pl.ds(4 * step + jj, L, stride=JD), :]
            flipped = jnp.transpose(block).astype(BF16)
            turned[64 * jj : 64 * jj + 64, :L] = flipped[:64]
            turned[64 * jj : 64 * jj + 64, L:] = flipped[64:]
        field = jnp.dot(turned[...], fourier_ref[...], preferred_element_type=F32)
        out_ref[pl.ds(4 * step, 4)] = field.astype(BF16).reshape(4, 64, NLON)
        return 0

    lax.fori_loop(0, JD // 4, body, 0)


def kernel(
    inputs_hbm,
    cotangent_hbm,
    weight_hbm,
    fourier_hbm,
    constants_hbm,
    field_ref,
    weight_grad_ref,
    inputs_ref,
    cotangent_ref,
    weight_ref,
    fourier_ref,
    seed_ref,
    unscale_ref,
    cos_ref,
    quad_wide,
    quad_ref,
    table_ref,
    gathered,
    matrices,
    near_out,
    near_in,
    field_out,
    field_in,
    grid_in,
    degree_out,
    degree_in,
    partial_out,
    partial_in,
    turned,
    pool,
    loaded,
    order_sent,
    order_got,
    degree_sent,
    degree_got,
    z_sent,
    z_got,
):
    z, y, dp = position()
    lat_rank = (z // 2) * 4 + y
    me_order = lat_rank * 2 + lax.rem(z, 2)
    me_degree = y * 8 + dp
    mesh_ids = pl.DeviceIdType.MESH
    wide = pool.at[pl.ds(0, OWNERS * 288)]
    packed_a = pool.at[pl.ds(OWNERS * 288, OWNERS * ALL_ROWS)]
    packed_b = pool.at[pl.ds(OWNERS * (288 + ALL_ROWS), OWNERS * ALL_ROWS)]
    order_rows = [(slots[0] * JD, len(slots) * JD) for slots in SETS]

    loads = [
        (cotangent_hbm, cotangent_ref),
        (fourier_hbm, fourier_ref),
        (weight_hbm, weight_ref),
        (inputs_hbm, inputs_ref),
        (constants_hbm.at[pl.ds(pl.multiple_of(me_order * 32, 32), 16)], seed_ref),
        (constants_hbm.at[pl.ds(pl.multiple_of(me_order * 32 + 16, 16), 16)], unscale_ref),
        (constants_hbm.at[pl.ds(OWNERS * 32, 16)], cos_ref),
        (constants_hbm.at[pl.ds(OWNERS * 32 + 16, 128)], quad_wide),
    ]
    loads = [pltpu.make_async_copy(a, b, loaded.at[n]) for n, (a, b) in enumerate(loads)]

    def order_peer(t):
        at = lax.rem(t * 13, 32)
        return lax.rem(z + lax.rem(at, 8), 8), lax.rem(y + at // 8, 4)

    def degree_peer(t):
        at = lax.rem(t * 13, 32)
        return lax.rem(y + lax.rem(at, 4), 4), lax.rem(dp + at // 4, 8)

    def order_copy(n, src, dst, t, first=0, rows=288):
        pz, py = order_peer(t)
        return pltpu.make_async_remote_copy(
            src_ref=src.at[((pz // 2) * 4 + py) * 2 + lax.rem(pz, 2), pl.ds(first, rows)],
            dst_ref=dst.at[me_order, pl.ds(first, rows)],
            send_sem=order_sent.at[n, t],
            recv_sem=order_got.at[n, t],
            device_id=place(pz, py, dp),
            device_id_type=mesh_ids,
        )

    def cotangent_copy(t):
        return order_copy(0, near_out, near_in, t)

    def field_copy(t):
        return order_copy(1, field_out, field_in, t)

    def grid_copy(number, t):
        return order_copy(2 + number, near_out, grid_in, t, *order_rows[number])

    def degree_copy(n, number, t):
        py, pd = degree_peer(t)
        return pltpu.make_async_remote_copy(
            src_ref=degree_out.at[n, py * 8 + pd, pl.ds(SET_ROWS * number, SET_ROWS)],
            dst_ref=degree_in.at[n, me_degree, pl.ds(SET_ROWS * number, SET_ROWS)],
            send_sem=degree_sent.at[2 * n + number, t],
            recv_sem=degree_got.at[2 * n + number, t],
            device_id=place(z, py, pd),
            device_id_type=mesh_ids,
        )

    def weight_copies(step):
        copies = []
        for sign, last, base in ((1, 4, 0), (-1, 3, 4)):
            if step > last:
                continue
            block = lax.rem(z + 8 - sign * (step - 1), 8)
            copies.append(
                pltpu.make_async_remote_copy(
                    src_ref=gathered.at[block],
                    dst_ref=gathered.at[block],
                    send_sem=z_sent.at[0, base + step],
                    recv_sem=z_got.at[0, base + step],
                    device_id=place(lax.rem(z + 8 + sign, 8), y, dp),
                    device_id_type=mesh_ids,
                )
            )
        return copies

    def forward_weights(step):
        if step > 1:
            for copy in weight_copies(step - 1):
                copy.wait_recv()
        for copy in weight_copies(step):
            copy.start()

    def partial_copy(t):
        pz = lax.rem(z + t, 8)
        return pltpu.make_async_remote_copy(
            src_ref=partial_out.at[pz],
            dst_ref=partial_in.at[z],
            send_sem=z_sent.at[1, t],
            recv_sem=z_got.at[1, t],
            device_id=place(pz, y, dp),
            device_id_type=mesh_ids,
        )

    def each(first, end, action):
        def body(t, _):
            action(t)
            return 0

        lax.fori_loop(first, end, body, 0)

    def send_field(first, end):
        each(first + 1, end + 1, lambda t: field_copy(t).start())

    def send_grid(number, first, end):
        each(first + 1, end + 1, lambda t: grid_copy(number, t).start())

    def send_degrees(n, number):
        each(1, 32, lambda t: degree_copy(n, number, t).start())
        rows = slice(SET_ROWS * number, SET_ROWS * number + SET_ROWS)
        degree_in[n, me_degree, rows, :] = degree_out[n, me_degree, rows, :]

    def wait_degrees(n, number):
        each(1, 32, lambda t: degree_copy(n, number, t).wait())

    def keep_grid(number):
        first, rows = order_rows[number]
        grid_in[me_order, first : first + rows, :] = near_out[me_order, first : first + rows, :]

    def factor_of(k):
        base = 1.0 / math.sqrt(NLAT)
        return jnp.where(me_order == 0, base, 2.0 * base) if k == 0 else 2.0 * base

    for load in loads:
        load.start()
    barrier = pltpu.get_barrier_semaphore()

    def greet(t):
        pz, py = order_peer(t)
        pl.semaphore_signal(barrier, inc=1, device_id=place(pz, py, dp), device_id_type=mesh_ids)
        py, pd = degree_peer(t)
        pl.semaphore_signal(barrier, inc=1, device_id=place(z, py, pd), device_id_type=mesh_ids)

    each(1, 32, greet)
    loads[2].wait()
    pl.semaphore_wait(barrier, 62)
    gathered[z] = weight_ref[...]
    forward_weights(1)
    loads[0].wait()
    loads[1].wait()

    transform(cotangent_ref, fourier_ref, wide, None, 0, 5)
    forward_weights(2)
    transform(cotangent_ref, fourier_ref, wide, None, 5, 9)
    forward_weights(3)
    transform(cotangent_ref, fourier_ref, wide, None, 9, JD // 2)
    narrow(wide, near_out, 288, 0, 288)
    forward_weights(4)
    each(1, 32, lambda t: cotangent_copy(t).start())
    near_in[me_order] = near_out[me_order]
    for load in loads[3:]:
        load.wait()
    for c in range(3):
        quad_ref[128 * c : 128 * c + 128, :] = quad_wide[:, 128 * c : 128 * c + 128]
    legendre(me_order, seed_ref, unscale_ref, cos_ref, table_ref, pool)
    transform(
        inputs_ref,
        fourier_ref,
        wide,
        lambda j: quad_ref[pl.ds(lat_rank * JD + j, 1), :],
        0,
        JD // 2,
    )
    narrow(wide, field_out, 288, 0, 288)
    field_in[me_order] = field_out[me_order]
    send_field(0, FIELD_SENT[0])
    for step in range(1, 5):
        for copy in weight_copies(step):
            copy.wait_send()
    for copy in weight_copies(4):
        copy.wait_recv()
    mixing_matrices(gathered, matrices)
    packed_a[...] = jnp.zeros((OWNERS * ALL_ROWS, 128), F32)
    packed_b[...] = jnp.zeros((OWNERS * ALL_ROWS, 128), F32)
    each(1, 32, lambda t: cotangent_copy(t).wait())

    widen(near_in, wide, 288, 0, 288)
    analyse(0, wide, table_ref, factor_of, degree_out.at[0], packed_a)
    send_degrees(0, 0)
    send_field(FIELD_SENT[0], FIELD_SENT[1])
    analyse(1, wide, table_ref, factor_of, degree_out.at[0], packed_a)
    send_degrees(0, 1)
    send_field(FIELD_SENT[1], FIELD_SENT[2])
    wait_degrees(0, 0)
    mix(0, degree_in.at[0], matrices, degree_out.at[1], packed_b, packed_a)
    send_degrees(1, 0)
    send_field(FIELD_SENT[2], FIELD_SENT[3])
    wait_degrees(0, 1)
    mix(1, degree_in.at[0], matrices, degree_out.at[1], packed_b, packed_a)
    send_degrees(1, 1)
    send_field(FIELD_SENT[3], FIELD_SENT[4])
    wait_degrees(1, 0)
    synthesise(0, degree_in.at[1], table_ref, quad_ref, near_out, packed_b, wide)
    send_field(FIELD_SENT[4], 31)
    send_grid(0, 0, 31)
    keep_grid(0)
    wait_degrees(1, 1)
    synthesise(1, degree_in.at[1], table_ref, quad_ref, near_out, packed_b, wide)
    send_grid(1, 0, GRID_SENT[0])
    keep_grid(1)

    each(1, 32, lambda t: field_copy(t).wait())
    widen(field_in, wide, 288, 0, 288)
    analyse(0, wide, table_ref, None, degree_out.at[2], packed_a)
    send_degrees(2, 0)
    send_grid(1, GRID_SENT[0], GRID_SENT[1])
    analyse(1, wide, table_ref, None, degree_out.at[2], packed_a)
    send_degrees(2, 1)
    send_grid(1, GRID_SENT[1], GRID_SENT[2])
    widen(degree_in.at[0], packed_b, ALL_ROWS, 0, ALL_ROWS)
    wait_degrees(2, 0)
    wait_degrees(2, 1)
    send_grid(1, GRID_SENT[2], 31)
    widen(degree_in.at[2], packed_a, ALL_ROWS, 0, ALL_ROWS)
    weight_grads(packed_a, packed_b, partial_out)
    each(1, 8, lambda t: partial_copy(t).start())
    partial_in[z] = partial_out[z]
    each(1, 32, lambda t: grid_copy(0, t).wait())
    each(1, 32, lambda t: grid_copy(1, t).wait())
    inverse(grid_in, fourier_ref, field_ref, wide, turned)
    each(1, 8, lambda t: partial_copy(t).wait())
    total = partial_in[0].astype(F32)
    for n in range(1, 8):
        total = total + partial_in[n].astype(F32)
    weight_grad_ref[...] = total


def shards(inputs, cotangent, weight):
    lat = np.arange(NLAT, dtype=np.float64)
    angle = math.pi * (lat + 0.5) / NLAT
    quad = (2.0 * math.pi * np.sin(angle) / math.sqrt(NLAT)).astype(np.float32)
    quad = np.repeat(quad.reshape(3, 128).T, 128, axis=1)
    cosine = np.broadcast_to(np.cos(angle).astype(np.float32)[None, :], (16, NLAT))
    constants = np.concatenate([legendre_seeds(), cosine, quad], axis=0)
    vmem = pl.BlockSpec(memory_space=pltpu.VMEM)
    anywhere = pl.BlockSpec(memory_space=pl.ANY)
    chunks = pltpu.VMEM((OWNERS, 288, 128), BF16)
    degrees = pltpu.VMEM((3, OWNERS, ALL_ROWS, 128), BF16)
    dma = pltpu.SemaphoreType.DMA
    field, weight_grad = pl.pallas_call(
        kernel,
        in_specs=[anywhere] * 5,
        out_specs=[vmem, vmem],
        out_shape=[
            jax.ShapeDtypeStruct((JD, 64, NLON), BF16),
            jax.ShapeDtypeStruct((L, 128), F32),
        ],
        scratch_shapes=[
            pltpu.VMEM((JD, 64, NLON), BF16),
            pltpu.VMEM((JD, 64, NLON), BF16),
            pltpu.VMEM((L, 128), BF16),
            pltpu.VMEM((2 * L, NLON), BF16),
            pltpu.VMEM((16, NLAT), F32),
            pltpu.VMEM((16, NLAT), F32),
            pltpu.VMEM((16, NLAT), F32),
            pltpu.VMEM((128, NLAT), F32),
            pltpu.VMEM((NLAT, 128), F32),
            pltpu.VMEM((SLOTS * L, NLAT), BF16),
            pltpu.VMEM((8, L, 128), BF16),
            pltpu.VMEM((12, 256, 256), BF16),
            chunks,
            chunks,
            chunks,
            chunks,
            chunks,
            degrees,
            degrees,
            pltpu.VMEM((8, L, 128), BF16),
            pltpu.VMEM((8, L, 128), BF16),
            pltpu.VMEM((256, 2 * L), BF16),
            pltpu.VMEM((OWNERS * (288 + 2 * ALL_ROWS), 128), F32),
            dma((8,)),
            dma((4, 32)),
            dma((4, 32)),
            dma((6, 32)),
            dma((6, 32)),
            dma((2, 8)),
            dma((2, 8)),
        ],
        compiler_params=pltpu.CompilerParams(
            vmem_limit_bytes=60 * MIB, collective_id=1, has_side_effects=True
        ),
        cost_estimate=pl.CostEstimate(
            flops=13_000_000_000, bytes_accessed=16_000_000, transcendentals=0
        ),
        name="sphere",
    )(
        inputs[0],
        cotangent[0],
        weight.reshape(L, 128),
        jnp.asarray(fourier_rows()),
        jnp.asarray(constants),
    )
    return field[None], weight_grad.reshape(3, 2, 64, 128)


def solution(mesh):
    fine = Mesh(mesh.devices.reshape(4, 4, 2, 8), ("zh", "y", "lon", "dp"))
    field = P("dp", ("zh", "y"), "lon", None)
    spectral = P(("zh", "y", "dp"), None, "lon", None)
    return jax.shard_map(
        shards,
        mesh=fine,
        in_specs=(field, field, spectral),
        out_specs=(field, spectral),
        check_vma=False,
    )
```

```python
import math

import jax
import jax.numpy as jnp
import numpy as np
from jax import lax
from jax.experimental import pallas as pl
from jax.experimental.pallas import tpu as pltpu
from jax.sharding import Mesh
from jax.sharding import PartitionSpec as P

L = 384
NLON = 768
NLAT = 384
C = 128
OWNERS = 32
SLOTS = 12
JD = 24
MIB = 1024 * 1024
F32 = jnp.float32
BF16 = jnp.bfloat16


def order_of(owner, slot):
    half = slot // 2
    return 64 * half + owner if slot % 2 == 0 else 64 * half + 63 - owner


SETS = (range(0, 4), range(4, SLOTS))
SET_ROWS = 96
FIELD_SENT = (8, 16, 24, 31, 31)
GRID_SENT = (8, 8, 31)
HALF_ROWS = 48
ALL_ROWS = 192


def row_index():
    table = {}
    for number, slots in enumerate(SETS):
        count = 0
        for slot in slots:
            for group in range(slot // 3, 4):
                for i in range(3):
                    for lon in range(2):
                        table[slot, group, i, lon] = SET_ROWS * number + HALF_ROWS * lon + count
                    count += 1
    return table


ROWS = row_index()


def fourier_rows():
    orders = np.array([order_of(o, k) for o in range(OWNERS) for k in range(SLOTS)], np.int64)
    phase = (orders[:, None] * np.arange(NLON)[None, :] % NLON) * (2.0 * math.pi / NLON)
    rows = np.concatenate([np.cos(phase), -np.sin(phase)], axis=0) / math.sqrt(NLON)
    return rows.astype(np.float32).astype(jnp.bfloat16)


def legendre_seeds():
    lat = np.arange(NLAT, dtype=np.float64)
    sine = np.sin(math.pi * (lat + 0.5) / NLAT)
    steps = np.arange(1, L, dtype=np.float64)
    cumlog = np.concatenate([np.zeros(1), np.cumsum(np.log1p(-0.5 / steps))])
    orders = np.array(
        [[min(order_of(o, k), L - 1) for k in range(16)] for o in range(OWNERS)], np.int64
    )
    m = orders[:, :, None].astype(np.float64)
    log_start = 0.5 * (
        np.log(2.0 * m + 1.0) - math.log(4.0 * math.pi) + cumlog[orders][:, :, None]
    ) + m * np.log(sine)[None, None, :]
    shift = np.clip(-log_start - 60.0, 0.0, 80.0)
    seed = np.exp(log_start + shift)
    seed = np.where(seed < 1.2e-38, 0.0, seed)
    return np.concatenate([seed, np.exp(-shift)], axis=1).astype(np.float32).reshape(-1, NLAT)


def low_half(shape):
    return lax.broadcasted_iota(jnp.int32, shape, len(shape) - 1) < 64


def position():
    z = lax.axis_index("zh") * 2 + lax.axis_index("lon")
    return z, lax.axis_index("y"), lax.axis_index("dp")


def place(z, y, dp):
    return (z // 2, y, lax.rem(z, 2), dp)


def widen(src_ref, held, stride, first, rows):
    def body(o, _):
        start = pl.multiple_of(o * stride + first, 16)
        held[pl.ds(start, rows), :] = src_ref[o, first : first + rows, :].astype(F32)
        return 0

    lax.fori_loop(0, OWNERS, body, 0)


def narrow(held, out_ref, stride, first, rows):
    def body(o, _):
        start = pl.multiple_of(o * stride + first, 16)
        out_ref[o, first : first + rows, :] = held[pl.ds(start, rows), :].astype(BF16)
        return 0

    lax.fori_loop(0, OWNERS, body, 0)


def transform(x_ref, fourier_ref, held, scale_of, first, end):
    low = low_half((L, 128))

    def body(step, _):
        x = x_ref[pl.ds(2 * step, 2)].reshape(128, NLON)
        spec = lax.dot_general(
            fourier_ref[...], x, (((1,), (1,)), ((), ())), preferred_element_type=F32
        )
        real, imag = spec[:L], spec[L:]
        even = jnp.where(low, real, pltpu.roll(imag, 64, 1))
        odd = jnp.where(low, pltpu.roll(real, 64, 1), imag)
        if scale_of is not None:
            even = even * scale_of(2 * step)
            odd = odd * scale_of(2 * step + 1)
        held[pl.ds(2 * step, L, stride=JD), :] = even
        held[pl.ds(2 * step + 1, L, stride=JD), :] = odd
        return 0

    lax.fori_loop(first, end, body, 0)


def legendre(owner, seed_ref, unscale_ref, cos_ref, out_ref, pool):
    slot = lax.broadcasted_iota(jnp.int32, (16, 128), 0)
    half = 64 * (slot // 2)
    order = jnp.where(lax.rem(slot, 2) == 0, half + owner, half + 63 - owner)
    order = jnp.minimum(order, L - 1)
    order_f = order.astype(F32)
    square = order_f * order_f
    cosine = cos_ref[...]

    def advance(degree, row, previous, before):
        degree_f = jnp.full((16, 128), degree, jnp.int32).astype(F32)
        up = jnp.sqrt(
            jnp.maximum(4.0 * degree_f * degree_f - 1.0, 1.0)
            / jnp.maximum(degree_f * degree_f - square, 1.0)
        )
        lower = degree_f - 1.0
        down = jnp.sqrt(
            jnp.maximum(lower * lower - square, 0.0)
            / jnp.maximum(4.0 * lower * lower - 1.0, 1.0)
        )
        fresh = []
        for c in range(3):
            lanes = slice(128 * c, 128 * c + 128)
            value = up * (cosine[:, lanes] * previous[c] - down * before[c])
            value = jnp.where(order == degree, seed_ref[:, lanes], value)
            value = jnp.where(order > degree, 0.0, value)
            pool[pl.ds(16 * L * c + row, 16, stride=L), :] = value * unscale_ref[:, lanes]
            fresh.append(value)
        return fresh, previous

    def body(step, carry):
        previous, before = list(carry[:3]), list(carry[3:])
        group = step // 32
        d = step - 32 * group
        for i in range(3):
            previous, before = advance(3 * step + i, 96 * group + 32 * i + d, previous, before)
        return tuple(previous) + tuple(before)

    zero = jnp.zeros((16, 128), F32)
    lax.fori_loop(0, L // 3, body, (zero,) * 6)

    def convert(k, _):
        start = pl.multiple_of(k * L, L)
        for c in range(3):
            out_ref[pl.ds(start, L), 128 * c : 128 * c + 128] = pool[
                pl.ds(16 * L * c + start, L), :
            ].astype(BF16)
        return 0

    lax.fori_loop(0, SLOTS, convert, 0)


def mixing_matrices(gathered_ref, out_ref):
    low = low_half((64, 128))
    for group in range(4):
        for i in range(3):
            for lon in range(2):
                source = gathered_ref[2 * group + lon, 128 * i : 128 * i + 128, :].astype(F32)
                real, imag = source[:64], source[64:]
                real_t, imag_t = pltpu.roll(real, 64, 1), pltpu.roll(imag, 64, 1)
                n, at = group * 3 + i, 128 * lon
                out_ref[n, at : at + 64, :128] = jnp.where(low, real, imag_t).astype(BF16)
                out_ref[n, at : at + 64, 128:] = jnp.where(low, real_t, imag).astype(BF16)
                out_ref[n, at + 64 : at + 128, :128] = jnp.where(low, -imag, real_t).astype(BF16)
                out_ref[n, at + 64 : at + 128, 128:] = jnp.where(low, -imag_t, real).astype(BF16)


def analyse(number, field, table_ref, factor_of, out_ref, packed):
    for k in SETS[number]:
        first = k // 3
        columns = []
        for lon in range(2):
            pieces = [
                field[(2 * s + lon) * 288 + k * JD : (2 * s + lon) * 288 + k * JD + JD, :]
                for s in range(16)
            ]
            columns.append(jnp.concatenate(pieces, axis=0).astype(BF16))
        data = jnp.concatenate(columns, axis=1)
        rows = table_ref[k * L + 96 * first : (k + 1) * L, :]
        result = jnp.dot(rows, data, preferred_element_type=F32)
        if factor_of is not None:
            result = result * factor_of(k)
        for group in range(first, 4):
            for i in range(3):
                at = ((group - first) * 3 + i) * 32
                for lon in range(2):
                    packed[pl.ds(ROWS[k, group, i, lon], 32, stride=ALL_ROWS), :] = result[
                        at : at + 32, 128 * lon : 128 * lon + 128
                    ]
    narrow(packed, out_ref, ALL_ROWS, SET_ROWS * number, SET_ROWS)


def degree_rows(held, slots, group, i):
    parts = []
    for lon in range(2):
        pieces = [held[pl.ds(ROWS[k, group, i, lon], 32, stride=ALL_ROWS), :] for k in slots]
        parts.append(jnp.concatenate(pieces, axis=0).astype(BF16))
    return jnp.concatenate(parts, axis=1)


def mix(number, grad_ref, matrix_ref, out_ref, held, packed):
    widen(grad_ref, held, ALL_ROWS, SET_ROWS * number, SET_ROWS)
    for group in range(4):
        slots = [k for k in SETS[number] if k // 3 <= group]
        if not slots:
            continue
        for i in range(3):
            mixed = lax.dot_general(
                degree_rows(held, slots, group, i),
                matrix_ref[group * 3 + i],
                (((1,), (1,)), ((), ())),
                preferred_element_type=F32,
            )
            for n, k in enumerate(slots):
                for lon in range(2):
                    packed[pl.ds(ROWS[k, group, i, lon], 32, stride=ALL_ROWS), :] = mixed[
                        32 * n : 32 * n + 32, 128 * lon : 128 * lon + 128
                    ]
    narrow(packed, out_ref, ALL_ROWS, SET_ROWS * number, SET_ROWS)


def weight_grads(held_c, held_g, out_ref):
    low = low_half((64, 128))
    for group in range(4):
        for i in range(3):
            slots = range(3 * group + 3)
            product = lax.dot_general(
                degree_rows(held_c, slots, group, i),
                degree_rows(held_g, slots, group, i),
                (((0,), (0,)), ((), ())),
                preferred_element_type=F32,
            ) * 0.125
            for lon in range(2):
                turned = []
                for half in range(2):
                    lanes = slice(128 * half, 128 * half + 128)
                    with_real = product[128 * lon : 128 * lon + 64, lanes]
                    with_imag = pltpu.roll(product[128 * lon + 64 : 128 * lon + 128, lanes], 64, 1)
                    turned.append(jnp.where(low, with_real + with_imag, with_real - with_imag))
                first, second = turned
                out_ref[2 * group + lon, 128 * i : 128 * i + 64, :] = jnp.where(
                    low, first, pltpu.roll(second, 64, 1)
                ).astype(BF16)
                out_ref[2 * group + lon, 128 * i + 64 : 128 * i + 128, :] = jnp.where(
                    low, pltpu.roll(first, 64, 1), second
                ).astype(BF16)


def synthesise(number, mixed_ref, table_ref, quad_ref, out_ref, held, grid):
    widen(mixed_ref, held, ALL_ROWS, SET_ROWS * number, SET_ROWS)
    for k in SETS[number]:
        first = k // 3
        parts = []
        for lon in range(2):
            pieces = [
                held[pl.ds(ROWS[k, group, i, lon], 32, stride=ALL_ROWS), :]
                for group in range(first, 4)
                for i in range(3)
            ]
            parts.append(jnp.concatenate(pieces, axis=0).astype(BF16))
        data = jnp.concatenate(parts, axis=1)
        rows = table_ref[k * L + 96 * first : (k + 1) * L, :]
        result = lax.dot_general(
            rows, data, (((0,), (0,)), ((), ())), preferred_element_type=F32
        )
        for lon in range(2):
            scaled = result[:, 128 * lon : 128 * lon + 128] * quad_ref[...]
            for s in range(16):
                at = (2 * s + lon) * 288 + k * JD
                grid[at : at + JD, :] = scaled[s * JD : s * JD + JD]
    slots = SETS[number]
    narrow(grid, out_ref, 288, slots[0] * JD, len(slots) * JD)


def inverse(spec_ref, fourier_ref, out_ref, held, turned):
    widen(spec_ref, held, 288, 0, 288)

    def body(step, _):
        for jj in range(4):
            block = held[pl.ds(4 * step + jj, L, stride=JD), :]
            flipped = jnp.transpose(block).astype(BF16)
            turned[64 * jj : 64 * jj + 64, :L] = flipped[:64]
            turned[64 * jj : 64 * jj + 64, L:] = flipped[64:]
        field = jnp.dot(turned[...], fourier_ref[...], preferred_element_type=F32)
        out_ref[pl.ds(4 * step, 4)] = field.astype(BF16).reshape(4, 64, NLON)
        return 0

    lax.fori_loop(0, JD // 4, body, 0)


def kernel(
    inputs_hbm,
    cotangent_hbm,
    weight_hbm,
    fourier_hbm,
    constants_hbm,
    field_hbm,
    weight_grad_ref,
    field_ref,
    inputs_ref,
    cotangent_ref,
    weight_ref,
    fourier_ref,
    seed_ref,
    unscale_ref,
    cos_ref,
    quad_wide,
    quad_ref,
    table_ref,
    gathered,
    matrices,
    near_out,
    near_in,
    field_out,
    field_in,
    grid_in,
    degree_out,
    degree_in,
    partial_out,
    partial_in,
    turned,
    pool,
    loaded,
    order_sent,
    order_got,
    degree_sent,
    degree_got,
    z_sent,
    z_got,
):
    z, y, dp = position()
    lat_rank = (z // 2) * 4 + y
    me_order = lat_rank * 2 + lax.rem(z, 2)
    me_degree = y * 8 + dp
    mesh_ids = pl.DeviceIdType.MESH
    wide = pool.at[pl.ds(0, OWNERS * 288)]
    packed_a = pool.at[pl.ds(OWNERS * 288, OWNERS * ALL_ROWS)]
    packed_b = pool.at[pl.ds(OWNERS * (288 + ALL_ROWS), OWNERS * ALL_ROWS)]
    order_rows = [(slots[0] * JD, len(slots) * JD) for slots in SETS]

    loads = [
        (cotangent_hbm, cotangent_ref),
        (fourier_hbm, fourier_ref),
        (weight_hbm, weight_ref),
        (inputs_hbm, inputs_ref),
        (constants_hbm.at[pl.ds(pl.multiple_of(me_order * 32, 32), 16)], seed_ref),
        (constants_hbm.at[pl.ds(pl.multiple_of(me_order * 32 + 16, 16), 16)], unscale_ref),
        (constants_hbm.at[pl.ds(OWNERS * 32, 16)], cos_ref),
        (constants_hbm.at[pl.ds(OWNERS * 32 + 16, 128)], quad_wide),
    ]
    loads = [pltpu.make_async_copy(a, b, loaded.at[n]) for n, (a, b) in enumerate(loads)]

    def order_peer(t):
        at = lax.rem(t * 13, 32)
        return lax.rem(z + lax.rem(at, 8), 8), lax.rem(y + at // 8, 4)

    def degree_peer(t):
        at = lax.rem(t * 13, 32)
        return lax.rem(y + lax.rem(at, 4), 4), lax.rem(dp + at // 4, 8)

    def order_copy(n, src, dst, t, first=0, rows=288):
        pz, py = order_peer(t)
        return pltpu.make_async_remote_copy(
            src_ref=src.at[((pz // 2) * 4 + py) * 2 + lax.rem(pz, 2), pl.ds(first, rows)],
            dst_ref=dst.at[me_order, pl.ds(first, rows)],
            send_sem=order_sent.at[n, t],
            recv_sem=order_got.at[n, t],
            device_id=place(pz, py, dp),
            device_id_type=mesh_ids,
        )

    def cotangent_copy(t):
        return order_copy(0, near_out, near_in, t)

    def field_copy(t):
        return order_copy(1, field_out, field_in, t)

    def grid_copy(number, t):
        return order_copy(2 + number, near_out, grid_in, t, *order_rows[number])

    def degree_copy(n, number, t):
        py, pd = degree_peer(t)
        return pltpu.make_async_remote_copy(
            src_ref=degree_out.at[n, py * 8 + pd, pl.ds(SET_ROWS * number, SET_ROWS)],
            dst_ref=degree_in.at[n, me_degree, pl.ds(SET_ROWS * number, SET_ROWS)],
            send_sem=degree_sent.at[2 * n + number, t],
            recv_sem=degree_got.at[2 * n + number, t],
            device_id=place(z, py, pd),
            device_id_type=mesh_ids,
        )

    def weight_copies(step):
        copies = []
        for sign, last, base in ((1, 4, 0), (-1, 3, 4)):
            if step > last:
                continue
            block = lax.rem(z + 8 - sign * (step - 1), 8)
            copies.append(
                pltpu.make_async_remote_copy(
                    src_ref=gathered.at[block],
                    dst_ref=gathered.at[block],
                    send_sem=z_sent.at[0, base + step],
                    recv_sem=z_got.at[0, base + step],
                    device_id=place(lax.rem(z + 8 + sign, 8), y, dp),
                    device_id_type=mesh_ids,
                )
            )
        return copies

    def forward_weights(step):
        if step > 1:
            for copy in weight_copies(step - 1):
                copy.wait_recv()
        for copy in weight_copies(step):
            copy.start()

    def partial_copy(t):
        pz = lax.rem(z + t, 8)
        return pltpu.make_async_remote_copy(
            src_ref=partial_out.at[pz],
            dst_ref=partial_in.at[z],
            send_sem=z_sent.at[1, t],
            recv_sem=z_got.at[1, t],
            device_id=place(pz, y, dp),
            device_id_type=mesh_ids,
        )

    def each(first, end, action):
        def body(t, _):
            action(t)
            return 0

        lax.fori_loop(first, end, body, 0)

    def send_field(first, end):
        each(first + 1, end + 1, lambda t: field_copy(t).start())

    def send_grid(number, first, end):
        each(first + 1, end + 1, lambda t: grid_copy(number, t).start())

    def send_degrees(n, number):
        each(1, 32, lambda t: degree_copy(n, number, t).start())
        rows = slice(SET_ROWS * number, SET_ROWS * number + SET_ROWS)
        degree_in[n, me_degree, rows, :] = degree_out[n, me_degree, rows, :]

    def wait_degrees(n, number):
        each(1, 32, lambda t: degree_copy(n, number, t).wait())

    def keep_grid(number):
        first, rows = order_rows[number]
        grid_in[me_order, first : first + rows, :] = near_out[me_order, first : first + rows, :]

    def factor_of(k):
        base = 1.0 / math.sqrt(NLAT)
        return jnp.where(me_order == 0, base, 2.0 * base) if k == 0 else 2.0 * base

    for load in loads:
        load.start()
    barrier = pltpu.get_barrier_semaphore()

    def greet(t):
        pz, py = order_peer(t)
        pl.semaphore_signal(barrier, inc=1, device_id=place(pz, py, dp), device_id_type=mesh_ids)
        py, pd = degree_peer(t)
        pl.semaphore_signal(barrier, inc=1, device_id=place(z, py, pd), device_id_type=mesh_ids)

    each(1, 32, greet)
    loads[2].wait()
    pl.semaphore_wait(barrier, 62)
    gathered[z] = weight_ref[...]
    forward_weights(1)
    loads[0].wait()
    loads[1].wait()

    transform(cotangent_ref, fourier_ref, wide, None, 0, 5)
    forward_weights(2)
    transform(cotangent_ref, fourier_ref, wide, None, 5, 9)
    forward_weights(3)
    transform(cotangent_ref, fourier_ref, wide, None, 9, JD // 2)
    narrow(wide, near_out, 288, 0, 288)
    forward_weights(4)
    each(1, 32, lambda t: cotangent_copy(t).start())
    near_in[me_order] = near_out[me_order]
    for load in loads[3:]:
        load.wait()
    for c in range(3):
        quad_ref[128 * c : 128 * c + 128, :] = quad_wide[:, 128 * c : 128 * c + 128]
    legendre(me_order, seed_ref, unscale_ref, cos_ref, table_ref, pool)
    transform(
        inputs_ref,
        fourier_ref,
        wide,
        lambda j: quad_ref[pl.ds(lat_rank * JD + j, 1), :],
        0,
        JD // 2,
    )
    narrow(wide, field_out, 288, 0, 288)
    field_in[me_order] = field_out[me_order]
    send_field(0, FIELD_SENT[0])
    for step in range(1, 5):
        for copy in weight_copies(step):
            copy.wait_send()
    for copy in weight_copies(4):
        copy.wait_recv()
    mixing_matrices(gathered, matrices)
    packed_a[...] = jnp.zeros((OWNERS * ALL_ROWS, 128), F32)
    packed_b[...] = jnp.zeros((OWNERS * ALL_ROWS, 128), F32)
    each(1, 32, lambda t: cotangent_copy(t).wait())

    widen(near_in, wide, 288, 0, 288)
    analyse(0, wide, table_ref, factor_of, degree_out.at[0], packed_a)
    send_degrees(0, 0)
    send_field(FIELD_SENT[0], FIELD_SENT[1])
    analyse(1, wide, table_ref, factor_of, degree_out.at[0], packed_a)
    send_degrees(0, 1)
    send_field(FIELD_SENT[1], FIELD_SENT[2])
    wait_degrees(0, 0)
    mix(0, degree_in.at[0], matrices, degree_out.at[1], packed_b, packed_a)
    send_degrees(1, 0)
    send_field(FIELD_SENT[2], FIELD_SENT[3])
    wait_degrees(0, 1)
    mix(1, degree_in.at[0], matrices, degree_out.at[1], packed_b, packed_a)
    send_degrees(1, 1)
    send_field(FIELD_SENT[3], FIELD_SENT[4])
    wait_degrees(1, 0)
    synthesise(0, degree_in.at[1], table_ref, quad_ref, near_out, packed_b, wide)
    send_field(FIELD_SENT[4], 31)
    send_grid(0, 0, 31)
    keep_grid(0)
    wait_degrees(1, 1)
    synthesise(1, degree_in.at[1], table_ref, quad_ref, near_out, packed_b, wide)
    send_grid(1, 0, GRID_SENT[0])
    keep_grid(1)

    each(1, 32, lambda t: field_copy(t).wait())
    widen(field_in, wide, 288, 0, 288)
    analyse(0, wide, table_ref, None, degree_out.at[2], packed_a)
    send_degrees(2, 0)
    send_grid(1, GRID_SENT[0], GRID_SENT[1])
    analyse(1, wide, table_ref, None, degree_out.at[2], packed_a)
    send_degrees(2, 1)
    send_grid(1, GRID_SENT[1], GRID_SENT[2])
    widen(degree_in.at[0], packed_b, ALL_ROWS, 0, ALL_ROWS)
    wait_degrees(2, 0)
    wait_degrees(2, 1)
    send_grid(1, GRID_SENT[2], 31)
    widen(degree_in.at[2], packed_a, ALL_ROWS, 0, ALL_ROWS)
    weight_grads(packed_a, packed_b, partial_out)
    each(1, 8, lambda t: partial_copy(t).start())
    partial_in[z] = partial_out[z]
    each(1, 32, lambda t: grid_copy(0, t).wait())
    each(1, 32, lambda t: grid_copy(1, t).wait())
    inverse(grid_in, fourier_ref, field_ref, wide, turned)
    store = pltpu.make_async_copy(field_ref, field_hbm, loaded.at[0])
    store.start()
    each(1, 8, lambda t: partial_copy(t).wait())
    total = partial_in[0].astype(F32)
    for n in range(1, 8):
        total = total + partial_in[n].astype(F32)
    weight_grad_ref[...] = total
    store.wait()


def shards(inputs, cotangent, weight):
    lat = np.arange(NLAT, dtype=np.float64)
    angle = math.pi * (lat + 0.5) / NLAT
    quad = (2.0 * math.pi * np.sin(angle) / math.sqrt(NLAT)).astype(np.float32)
    quad = np.repeat(quad.reshape(3, 128).T, 128, axis=1)
    cosine = np.broadcast_to(np.cos(angle).astype(np.float32)[None, :], (16, NLAT))
    constants = np.concatenate([legendre_seeds(), cosine, quad], axis=0)
    vmem = pl.BlockSpec(memory_space=pltpu.VMEM)
    anywhere = pl.BlockSpec(memory_space=pl.ANY)
    chunks = pltpu.VMEM((OWNERS, 288, 128), BF16)
    degrees = pltpu.VMEM((3, OWNERS, ALL_ROWS, 128), BF16)
    dma = pltpu.SemaphoreType.DMA
    field, weight_grad = pl.pallas_call(
        kernel,
        in_specs=[anywhere] * 5,
        out_specs=[anywhere, vmem],
        out_shape=[
            jax.ShapeDtypeStruct((JD, 64, NLON), BF16),
            jax.ShapeDtypeStruct((L, 128), F32),
        ],
        scratch_shapes=[
            pltpu.VMEM((JD, 64, NLON), BF16),
            pltpu.VMEM((JD, 64, NLON), BF16),
            pltpu.VMEM((JD, 64, NLON), BF16),
            pltpu.VMEM((L, 128), BF16),
            pltpu.VMEM((2 * L, NLON), BF16),
            pltpu.VMEM((16, NLAT), F32),
            pltpu.VMEM((16, NLAT), F32),
            pltpu.VMEM((16, NLAT), F32),
            pltpu.VMEM((128, NLAT), F32),
            pltpu.VMEM((NLAT, 128), F32),
            pltpu.VMEM((SLOTS * L, NLAT), BF16),
            pltpu.VMEM((8, L, 128), BF16),
            pltpu.VMEM((12, 256, 256), BF16),
            chunks,
            chunks,
            chunks,
            chunks,
            chunks,
            degrees,
            degrees,
            pltpu.VMEM((8, L, 128), BF16),
            pltpu.VMEM((8, L, 128), BF16),
            pltpu.VMEM((256, 2 * L), BF16),
            pltpu.VMEM((OWNERS * (288 + 2 * ALL_ROWS), 128), F32),
            dma((8,)),
            dma((4, 32)),
            dma((4, 32)),
            dma((6, 32)),
            dma((6, 32)),
            dma((2, 8)),
            dma((2, 8)),
        ],
        compiler_params=pltpu.CompilerParams(
            vmem_limit_bytes=60 * MIB, collective_id=1, has_side_effects=True
        ),
        cost_estimate=pl.CostEstimate(
            flops=13_000_000_000, bytes_accessed=16_000_000, transcendentals=0
        ),
        name="sphere",
    )(
        inputs[0],
        cotangent[0],
        weight.reshape(L, 128),
        jnp.asarray(fourier_rows()),
        jnp.asarray(constants),
    )
    return field[None], weight_grad.reshape(3, 2, 64, 128)


def solution(mesh):
    fine = Mesh(mesh.devices.reshape(4, 4, 2, 8), ("zh", "y", "lon", "dp"))
    field = P("dp", ("zh", "y"), "lon", None)
    spectral = P(("zh", "y", "dp"), None, "lon", None)
    return jax.shard_map(
        shards,
        mesh=fine,
        in_specs=(field, field, spectral),
        out_specs=(field, spectral),
        check_vma=False,
    )
```
